256 devices in a mesh: tile: 64 (over y_hi, x, z), head: 4 (over y_lo, core).
Axes of the slice: x: 4, y: 4 (y_hi: 2, y_lo: 2; y = y_hi * 2 + y_lo), z: 8, core: 2. Of those that a mesh axis runs over, the one named last changes fastest.
Arguments:
- tokens: bfloat16 [4, 96, 768, 512], P(None, 'head', 'tile'), may hold values from -6 to 6
- land_sea: int32 [96, 768], P('head', 'tile'), may hold values 0 or 1
- land_embed: float32 [2, 512], replicated, may hold values from -6 to 6
- gain_attn: float32 [512], replicated, may hold values from 0.1 to 1.9
- qkv_weight: bfloat16 [3, 512, 512], P(None, None, 'head'), may hold values from -0.25 to 0.25
- out_weight: bfloat16 [512, 512], P('head'), may hold values from -0.25 to 0.25
- bias_left: bfloat16 [8, 144, 32], P('head'), may hold values from -10 to 10
- bias_right: bfloat16 [8, 144, 32], P('head'), may hold values from -10 to 10
- gain_mlp: float32 [512], replicated, may hold values from 0.1 to 1.9
- up_weight: bfloat16 [512, 2048], replicated, may hold values from -0.25 to 0.25
- down_weight: bfloat16 [2048, 512], replicated, may hold values from -0.125 to 0.125
Outputs:
- block_out: bfloat16 [4, 96, 768, 512], P(None, 'head', 'tile')
The draws below stay inside these ranges and needn't reach their ends.
All inputs are finite; a program needn't handle non-finite values. No bound on the sum of `land_sea` on one device may be relied on, other than what follows from the above.
Results may differ from the reference program's by a relative error of at most 0.011.
Values may be sent and summed in bfloat16 or wider, within the bound.
No kernel may reach another device: no remote copies, remote signals or barrier semaphores. Data moves between devices by JAX's collectives and lax.ppermute only.
A program may use at most 128 MiB of HBM per device.

```python
import jax
import jax.numpy as jnp
from jax import lax

D = 512
HEADS = 8
HS = 64
FFN = 2048
RANK = 32
WLV = 2
WLAT = 6
WLON = 12
WIN = 144
LEVELS = 4
LAT = 96
LON = 768


def draw_bias_left(key, part):
    key = jax.random.fold_in(key, 1)
    return jnp.clip(0.35 * jax.random.normal(key, (HEADS, WIN, RANK), jnp.float32), -1.5, 1.5).astype(jnp.bfloat16)


def draw_bias_right(key, part):
    key = jax.random.fold_in(key, 2)
    return jnp.clip(0.35 * jax.random.normal(key, (HEADS, WIN, RANK), jnp.float32), -1.5, 1.5).astype(jnp.bfloat16)


def set_ends(values, stream_key, smallest, largest):
    longest = values.shape.index(max(values.shape))
    spots = []
    for shift in (0, 1):
        where = [jax.random.randint(jax.random.fold_in(stream_key, axis), (), 0, length) for axis, length in enumerate(values.shape)]
        where[longest] = (where[longest] + shift) % values.shape[longest]
        spots.append(tuple(where))
    return values.at[spots[0]].set(smallest).at[spots[1]].set(largest)


def steps_of(own_key, shape, cuts, smallest, high):
    gain = 1.0
    for dim, shards_of in cuts:
        draws = jax.random.uniform(jax.random.fold_in(jax.random.fold_in(own_key, 6), dim), (shards_of,), jnp.float32, smallest / len(cuts), high / len(cuts))
        gain = gain * jnp.repeat(jnp.exp(draws), shape[dim] // shards_of).reshape((-1,) + (1,) * (len(shape) - 1 - dim))
    return gain


def gaussian(stream_key, shape, scale, reach, cuts=(), held_as=jnp.bfloat16):
    drawn = jax.random.normal(stream_key, shape, jnp.float32) * scale
    if len(cuts) > 0:
        drawn = steps_of(stream_key, shape, cuts, -0.22, 0.18) * drawn
    return jnp.clip(drawn, min=-reach, max=reach).astype(held_as)


def setup_inputs(seed: int = 0) -> dict:
    keys = jax.random.split(jax.random.key(seed), 12)
    tokens = gaussian(keys[0], (LEVELS, LAT, LON, D), 1.0, 6.0, ((1, 4), (2, 64)))
    land_sea = set_ends((jax.random.randint(keys[1], (LAT, LON), 0, 10) < 3).astype(jnp.int32), jax.random.fold_in(keys[1], 1), 0, 1)
    land_embed = gaussian(keys[2], (2, D), 1.0, 6.0, (), jnp.float32)
    gain_attn = jnp.clip(1.0 + 0.18 * jax.random.normal(keys[3], (D,), jnp.float32), 0.1, 1.9)
    qkv_weight = gaussian(keys[4], (3, D, D), D ** -0.5, 0.25, ((2, 4),))
    out_weight = gaussian(keys[5], (D, D), D ** -0.5, 0.25, ((0, 4),))
    bias_left = draw_bias_left(jax.random.fold_in(keys[11], 71), 0)
    bias_right = draw_bias_right(jax.random.fold_in(keys[11], 71), 0)
    gain_mlp = jnp.clip(1.0 + 0.18 * jax.random.normal(keys[8], (D,), jnp.float32), 0.1, 1.9)
    up_weight = gaussian(keys[9], (D, FFN), D ** -0.5, 0.25)
    down_weight = gaussian(keys[10], (FFN, D), FFN ** -0.5, 0.125)
    return dict(tokens=tokens, land_sea=land_sea, land_embed=land_embed, gain_attn=gain_attn, qkv_weight=qkv_weight, out_weight=out_weight, bias_left=bias_left, bias_right=bias_right, gain_mlp=gain_mlp, up_weight=up_weight, down_weight=down_weight)


def layer_norm(values, norm_gain):
    average = lax.optimization_barrier(jnp.mean(values, axis=-1, keepdims=True))
    centred = values - average
    variance = lax.optimization_barrier(jnp.mean(centred * centred, axis=-1, keepdims=True))
    return centred * lax.rsqrt(variance + 1e-05) * norm_gain.astype(jnp.float32)

def region_label(coords, extent, window):
    return (coords >= extent - window).astype(jnp.int32) + (coords >= extent - window // 2).astype(jnp.int32)

def to_windows(field_grid):
    level_count, row_count, col_count, features = field_grid.shape
    pieces = field_grid.reshape(level_count // WLV, WLV, row_count // WLAT, WLAT, col_count // WLON, WLON, features)
    return pieces.transpose(0, 2, 4, 1, 3, 5, 6).reshape(-1, WLV * WLAT * WLON, features)

def from_windows(blocks, level_count, row_count, col_count):
    features = blocks.shape[-1]
    pieces = blocks.reshape(level_count // WLV, row_count // WLAT, col_count // WLON, WLV, WLAT, WLON, features)
    return pieces.transpose(0, 3, 1, 4, 2, 5, 6).reshape(level_count, row_count, col_count, features)

def window_penalty(level_coords, lat_coords, lat_total, col_count):
    level_label = region_label(level_coords, LEVELS, WLV)
    lat_label = region_label(lat_coords, lat_total, WLAT)
    labels = level_label[:, None] * 3 + lat_label[None, :]
    labels = jnp.broadcast_to(labels[:, :, None, None], labels.shape + (col_count, 1))
    flattened = to_windows(labels)[:, :, 0]
    same = flattened[:, :, None] == flattened[:, None, :]
    return jnp.where(same, jnp.float32(0.0), jnp.float32(-1000000000.0)).astype(jnp.float32)

def project_qkv(row_grid, qkv_weight):
    product = jnp.einsum('abcd,tde->tabce', row_grid.astype(jnp.float32), qkv_weight.astype(jnp.float32))
    scaling = jnp.array([float(HS) ** (-0.5), 1.0, 1.0], jnp.float32)
    return (product * scaling[:, None, None, None, None]).astype(jnp.bfloat16)

def attend(qkv_grid, bias_left, bias_right, penalty, out_weight):
    query_block = to_windows(qkv_grid[0])
    key_block = to_windows(qkv_grid[1])
    value_block = to_windows(qkv_grid[2])
    head_count = bias_left.shape[0]
    head_dim = query_block.shape[-1] // head_count
    split_shape = query_block.shape[:2] + (head_count, head_dim)
    scores = jnp.einsum('wqhe,wkhe->whqk', query_block.reshape(split_shape).astype(jnp.float32), key_block.reshape(split_shape).astype(jnp.float32))
    position_bias = jnp.einsum('hqr,hkr->hqk', bias_left.astype(jnp.float32), bias_right.astype(jnp.float32))
    scores = scores + position_bias[None] + penalty[:, None]
    highest = lax.optimization_barrier(jnp.max(scores, axis=-1, keepdims=True))
    weights = jnp.exp(scores - highest)
    normed_weights = (weights / lax.optimization_barrier(jnp.sum(weights, axis=-1, keepdims=True))).astype(jnp.bfloat16)
    blended = jnp.einsum('whqk,wkhe->wqhe', normed_weights.astype(jnp.float32), value_block.reshape(split_shape).astype(jnp.float32)).astype(jnp.bfloat16)
    flat_heads = blended.reshape(query_block.shape).astype(jnp.float32)
    return jnp.einsum('wqd,de->wqe', flat_heads, out_weight.astype(jnp.float32))

def reference(tokens, land_sea, land_embed, gain_attn, qkv_weight, out_weight, bias_left, bias_right, gain_mlp, up_weight, down_weight):
    embed_rows = jnp.where(land_sea[None, :, :, None] == 1, land_embed[1].astype(jnp.float32), land_embed[0].astype(jnp.float32))
    resid = tokens.astype(jnp.float32) + embed_rows
    normed = layer_norm(resid, gain_attn).astype(jnp.bfloat16)
    rolled = jnp.roll(normed, (-1, -(WLAT // 2), -(WLON // 2)), axis=(0, 1, 2))
    penalty = window_penalty(jnp.arange(LEVELS, dtype=jnp.int32), jnp.arange(LAT, dtype=jnp.int32), LAT, WLON)
    group_count = LON // WLON

    def one_group(index):
        block = lax.dynamic_slice_in_dim(rolled, (index * WLON).astype(jnp.int32), WLON, 2)
        result = attend(project_qkv(block, qkv_weight), bias_left, bias_right, penalty, out_weight)
        return from_windows(result, LEVELS, LAT, WLON)
    pieces = lax.map(one_group, jnp.arange(group_count, dtype=jnp.int32))
    attended = jnp.transpose(pieces, (1, 2, 0, 3, 4)).reshape(LEVELS, LAT, LON, D)
    attended = jnp.roll(attended, (1, WLAT // 2, WLON // 2), axis=(0, 1, 2))
    mixed_resid = (resid + attended).reshape(LEVELS * LAT, LON, D)

    def mlp_row(row_block):
        second = layer_norm(row_block, gain_mlp).astype(jnp.bfloat16)
        hidden = jax.nn.gelu(jnp.dot(second, up_weight, preferred_element_type=jnp.float32), approximate=False).astype(jnp.bfloat16)
        return (row_block + jnp.dot(hidden, down_weight, preferred_element_type=jnp.float32)).astype(jnp.bfloat16)
    block_out = lax.map(mlp_row, mixed_resid)
    return block_out.reshape(LEVELS, LAT, LON, D)
```

```python
import functools

import jax
import jax.numpy as jnp
import numpy as np
from jax import lax
from jax.experimental import pallas as pl
from jax.experimental.pallas import tpu as pltpu
from jax.sharding import PartitionSpec as P

D = 512
AXES = ("tile", "head")
BF = jnp.bfloat16
F32 = jnp.float32
MIB = 2**20
PLACE = {1: (0, 0), 2: (0, 1), 3: (1, 0), 0: (1, 1)}
NT = (((1,), (1,)), ((), ()))
PENALTY = -1000000000.0
VMEM = pl.BlockSpec(memory_space=pltpu.VMEM)
SMEM = pl.BlockSpec(memory_space=pltpu.SMEM)
ANY = pl.BlockSpec(memory_space=pl.ANY)


def dot(left, right):
    return jnp.dot(left, right, preferred_element_type=F32)


def dot_nt(left, right):
    return lax.dot_general(left, right, NT, preferred_element_type=F32)


def layer_norm(values, norm_gain):
    average = jnp.mean(values, axis=-1, keepdims=True)
    centred = values - average
    variance = jnp.mean(centred * centred, axis=-1, keepdims=True)
    return centred * lax.rsqrt(variance + 1e-05) * norm_gain


def pack_kernel(wqkv, wo, left, right, up, down, whole):
    def put(row, count, value):
        whole[row : row + count, :] = value
        if row + count <= 1152:
            up[row : row + count, :] = value
        else:
            down[row - 1152 : row - 1152 + count, :] = value

    for start in range(0, 1536, 128):
        put(start, 128, wqkv[start : start + 128, :])
    for block in range(4):
        put(1536 + 128 * block, 128, wo[:, 128 * block : 128 * block + 128])
    for index, factor in enumerate((left, right)):
        base = 2048 + 128 * index
        put(base, 64, factor[:, :128])
        tail = jnp.concatenate((factor[:, 128:], jnp.zeros((64, 112), BF)), axis=1)
        put(base + 64, 64, tail)


def norm_kernel(flags, tokens, embed, gain, norm_a, norm_b, resid):
    parity = flags[0]
    for half in range(2):
        side = parity if half == 0 else 1 - parity
        base = 576 * half
        for level in range(4):
            pair, inner = PLACE[level]
            for col in range(6):
                row = tokens[level, side, col].astype(F32) + embed[side, col]
                for k in range(3):
                    at = base + (pair * 3 + k) * 72 + inner * 36 + col * 6
                    resid[at : at + 6, :] = row[3 + 6 * k : 9 + 6 * k, :]
                at = base + 432 + level * 18 + col * 3
                resid[at : at + 3, :] = row[:3, :]
                resid[at + 72 : at + 75, :] = row[21:, :]
        target = norm_a if half == 0 else norm_b
        for chunk in range(4):
            at = base + 144 * chunk
            target[144 * chunk : 144 * chunk + 144, :] = layer_norm(
                resid[at : at + 144, :], gain[...]
            ).astype(BF)


def repeat4(value):
    return jnp.concatenate((value,) * 4, axis=0)


def head_stack(value, width):
    lane = lax.broadcasted_iota(jnp.int32, value.shape, 1) // width
    return jnp.concatenate(
        [jnp.where(lane == head, value, 0.0) for head in range(4)], axis=0
    ).astype(BF)


def head_pick(stacked):
    lane = lax.broadcasted_iota(jnp.int32, (72, stacked.shape[1]), 1) // 64
    total = stacked[:72]
    for head in range(1, 4):
        total = jnp.where(lane == head, stacked[72 * head : 72 * head + 72], total)
    return total


def level_label(index):
    level = lax.rem(index, 72) // 18
    return jnp.where(level == 0, 2, jnp.where(level == 3, 1, 0))


def qkv_kernel(
    flags, norm_a, norm_b, own, mate, far_up, far_down, fwd_up, fwd_down, pos_query, pos_key,
    query, key, value, wkv, wo, bias_in, bias_edge, wq, left, right,
):
    def part(source, row, count):
        if source == 0:
            return own[row : row + count, :]
        if source == 1:
            return mate[row : row + count, :]
        first, second = ((far_up, far_down), (fwd_up, fwd_down))[source - 2]
        if row + count <= 1152:
            return first[row : row + count, :]
        return second[row - 1152 : row - 1152 + count, :]

    for source in range(4):
        lanes = slice(128 * source, 128 * source + 128)
        wq[:, lanes] = part(source, 0, 512)
        wkv[:, lanes] = part(source, 512, 512)
        more = slice(512 + 128 * source, 640 + 128 * source)
        wkv[:128, more] = part(source, 1024, 128)
        wkv[128:, more] = part(source, 1152, 384)
        for block in range(4):
            wo[lanes, 128 * block : 128 * block + 128] = part(source, 1536 + 128 * block, 128)
        rows = slice(64 * source, 64 * source + 64)
        left[rows, :128] = part(source, 2048, 64)
        left[rows, 128:] = part(source, 2112, 64)
        right[rows, :128] = part(source, 2176, 64)
        right[rows, 128:] = part(source, 2240, 64)
    for half, norm in enumerate((norm_a, norm_b)):
        for chunk in range(4):
            rows = norm[144 * chunk : 144 * chunk + 144, :]
            got_q = dot(rows, wq[...]) * 0.125
            got_kv = dot(rows, wkv[...])
            for sub in range(2):
                at = slice(72 * sub, 72 * sub + 72)
                query[half, 2 * chunk + sub] = got_q[at].astype(BF)
                key[half, 2 * chunk + sub] = got_kv[at, :512].astype(BF)
                value[half, 2 * chunk + sub] = got_kv[at, 512:].astype(BF)
    factors = dot_nt(pos_query[...], left[...])
    q_level = lax.broadcasted_iota(jnp.int32, (72, 144), 0) >= 36
    k_level = lax.rem(lax.broadcasted_iota(jnp.int32, (72, 144), 1), 72) >= 36
    split = repeat4(jnp.where(q_level == k_level, 0.0, PENALTY))
    q_label = level_label(lax.broadcasted_iota(jnp.int32, (72, 288), 0))
    k_index = lax.broadcasted_iota(jnp.int32, (72, 288), 1)
    apart = q_label != level_label(k_index)
    halo = lax.rem(k_index // 72, 2) == 1
    for group in range(2):
        lanes = slice(128 * group, 128 * group + 128)
        rows = slice(288 * group, 288 * group + 288)
        for half in range(2):
            own_rows = head_stack(factors[72 * half : 72 * half + 72, lanes], 32)
            keys = dot_nt(right[lanes, :], pos_key[144 * half : 144 * half + 144, :]).astype(BF)
            bias = dot(own_rows, keys)
            bias_in[half, 0, rows, :] = bias
            bias_in[half, 1, rows, :] = bias + split
            for side in range(2):
                at = 144 + 144 * half + 72 * (1 - side)
                own_rows = head_stack(factors[at : at + 72, lanes], 32)
                at = 288 + 576 * half + 288 * side
                keys = dot_nt(right[lanes, :], pos_key[at : at + 288, :]).astype(BF)
                outside = jnp.logical_and(halo, flags[1 + side] == 1)
                mask = jnp.where(jnp.logical_or(apart, outside), PENALTY, 0.0)
                bias_edge[half, side, rows, :] = dot(own_rows, keys) + repeat4(mask)


def attend(query, keys, values, bias):
    picked = []
    for group in range(2):
        lanes = slice(256 * group, 256 * group + 256)
        rows = slice(288 * group, 288 * group + 288)
        stacked = head_stack(query[:, lanes].astype(F32), 64)
        scores = dot_nt(stacked, keys[:, lanes]) + bias[rows, :]
        weights = jnp.exp(scores - jnp.max(scores, axis=-1, keepdims=True))
        weights = weights * (1.0 / jnp.sum(weights, axis=-1, keepdims=True))
        picked.append(head_pick(dot(weights.astype(BF), values[:, lanes])))
    return jnp.concatenate(picked, axis=1)


def feed_forward(heads_out, resid, wo, gain, up, down):
    mixed = resid + dot(heads_out.astype(BF), wo[...])
    second = layer_norm(mixed, gain[...]).astype(BF)
    inner = dot(second, up[...])
    hidden = (0.5 * inner * (1.0 + lax.erf(inner * 0.7071067811865476))).astype(BF)
    return mixed + dot(hidden, down[...])


def fetch(up_any, down_any, up, down, sems):
    copies = (
        pltpu.make_async_copy(up_any, up, sems.at[0]),
        pltpu.make_async_copy(down_any, down, sems.at[1]),
    )
    for copy in copies:
        copy.start()
    return copies


def half_kernel(
    remote, query, key, value, wkv, wo, bias, resid, gain, up_any, down_any,
    out, edge_key, edge_value, keys, values, heads, up, down, sems,
):
    copies = fetch(up_any, down_any, up, down, sems)
    for chunk in range(4):
        got = dot(remote[144 * chunk : 144 * chunk + 144, :], wkv[...])
        for sub in range(2):
            block = 2 * chunk + sub
            part = got[72 * sub : 72 * sub + 72]
            if block < 6:
                joined = jnp.concatenate((key[0, block].astype(F32), part[:, :512]), axis=0)
                keys[block] = joined.astype(BF)
                joined = jnp.concatenate((value[0, block].astype(F32), part[:, 512:]), axis=0)
                values[block] = joined.astype(BF)
            else:
                edge_key[block - 6] = part[:, :512].astype(BF)
                edge_value[block - 6] = part[:, 512:].astype(BF)
    for block in range(6):
        heads[72 * block : 72 * block + 72, :] = attend(
            query[0, block], keys[block], values[block], bias.at[0, block // 3]
        )
    for copy in copies:
        copy.wait()
    for chunk in range(3):
        rows = slice(144 * chunk, 144 * chunk + 144)
        out[rows, :] = feed_forward(heads[rows, :], resid[rows, :], wo, gain, up, down)


def edge_kernel(
    flags, below, below_a, above, above_a, query, key, value, key_a, value_a, key_b, value_b,
    wkv, wo, bias, resid, gain, out_a, out_b, up_any, down_any,
    out, halo, keys, values, heads, edges, grid, up, down, sems,
):
    copies = fetch(up_any, down_any, up, down, sems)
    parity = flags[0]
    for side, (first, second) in enumerate(((below, below_a), (above, above_a))):
        got = dot(first[...], wkv[...])
        for index in range(3):
            halo[side, index] = got[72 * index : 72 * index + 72]
        halo[side, 3] = dot(second[...], wkv[...])
    for half in range(2):
        remote_key, remote_value = ((key_a, value_a), (key_b, value_b))[half]
        near, far = ((0, 3), (1, 2))[half]
        for side in range(2):
            joined = (
                key[half, side].astype(F32), halo[side, near, :, :512],
                remote_key[side].astype(F32), halo[side, far, :, :512],
            )
            keys[...] = jnp.concatenate(joined, axis=0).astype(BF)
            joined = (
                value[half, side].astype(F32), halo[side, near, :, 512:],
                remote_value[side].astype(F32), halo[side, far, :, 512:],
            )
            values[...] = jnp.concatenate(joined, axis=0).astype(BF)
            at = 144 * half + 72 * side
            heads[at : at + 72, :] = attend(
                query[half, side], keys[...], values[...], bias.at[half, side]
            )
    for copy in copies:
        copy.wait()
    for half in range(2):
        rows = slice(144 * half, 144 * half + 144)
        edges[rows, :] = feed_forward(heads[rows, :], resid[half], wo, gain, up, down)
    for half, inside in enumerate((out_a, out_b)):
        side = parity if half == 0 else 1 - parity
        for level in range(4):
            pair, inner = PLACE[level]
            for col in range(6):
                at = 144 * half + level * 18 + col * 3
                grid[level, col, :3, :] = edges[at : at + 3, :]
                grid[level, col, 21:, :] = edges[at + 72 : at + 75, :]
                for k in range(3):
                    at = (pair * 3 + k) * 72 + inner * 36 + col * 6
                    grid[level, col, 3 + 6 * k : 9 + 6 * k, :] = inside[at : at + 6, :]
                out[level, side, col] = grid[level, col].astype(BF)


def call(kernel, out_shape, in_specs, scratch=(), limit=48, **extra):
    many = isinstance(out_shape, (list, tuple))
    return pl.pallas_call(
        kernel,
        out_shape=out_shape,
        in_specs=in_specs,
        out_specs=[VMEM] * len(out_shape) if many else VMEM,
        scratch_shapes=scratch,
        compiler_params=pltpu.CompilerParams(vmem_limit_bytes=limit * MIB),
        **extra,
    )


def shape(*dims, dtype=BF):
    return jax.ShapeDtypeStruct(dims, dtype)


def position_tables():
    tables = []
    for parity in range(2):
        columns = (1 - parity, parity)

        def inside(half):
            c = columns[half]
            return [l * 72 + r * 12 + 6 * c + col for l in range(2) for col in range(6) for r in range(6)]

        def edge(half, rows):
            c = columns[half]
            return [
                PLACE[l][1] * 72 + (3 * rows + r) * 12 + 6 * c + col
                for l in range(4) for col in range(6) for r in range(3)
            ]

        query = inside(0) + inside(1)
        for half in range(2):
            query += edge(half, 0) + edge(half, 1)
        key = []
        for half in range(2):
            key += inside(half) + inside(1 - half)
        for half in range(2):
            for side in range(2):
                near = 1 - side
                for h in (half, 1 - half):
                    key += edge(h, near) + edge(h, 1 - near)
        tables.append(query + key)
    return np.array(tables, np.int32)


def pairs_of(tiles, move):
    pairs = []
    for tile in range(tiles):
        for head in range(4):
            target = move(tile, head)
            if target is not None:
                pairs.append((tile * 4 + head, (target[0] % tiles) * 4 + target[1]))
    return pairs


def shards(
    tokens, land_sea, land_embed, gain_attn, qkv_weight, out_weight, bias_left, bias_right,
    gain_mlp, up_weight, down_weight,
):
    tiles = lax.axis_size("tile")
    tile, head = lax.axis_index("tile"), lax.axis_index("head")
    parity = lax.rem(tile, 2)

    def along_y(steps):
        def move(t, h):
            high, rest = divmod(t, tiles // 2)
            y = (2 * high + h // 2 + steps) % 4
            return (y // 2) * (tiles // 2) + rest, (y % 2) * 2 + h % 2

        return move

    def send(value, move):
        return lax.ppermute(value, AXES, pairs_of(tiles, move))

    swap_a = lambda t, h: (t + 1 if t % 2 else t - 1, h)
    swap_b = lambda t, h: (t ^ 1, h)
    swap_core = lambda t, h: (t, h ^ 1)
    to_next = lambda t, h: (t, h + 1) if h < 3 else None
    to_last = lambda t, h: (t, h - 1) if h > 0 else None

    flags = jnp.stack((parity, (head == 0).astype(jnp.int32), (head == 3).astype(jnp.int32)))
    flags = flags.astype(jnp.int32)

    pack_up, pack_down, pack = call(
        pack_kernel, [shape(1152, 128), shape(1152, 128), shape(2304, 128)], [VMEM] * 4, name="pack"
    )(
        qkv_weight.reshape(1536, 128),
        out_weight,
        bias_left.transpose(0, 2, 1).reshape(64, 144),
        bias_right.transpose(0, 2, 1).reshape(64, 144),
    )
    far_up = send(pack_up, along_y(1))
    far_down = send(pack_down, along_y(-1))
    mate = send(pack, swap_core)

    grid = tokens.transpose(0, 2, 1, 3).reshape(4, 2, 6, 24, D)
    land = land_sea.transpose(1, 0)[:, :, None]
    embed = jnp.where(land == 1, land_embed[1], land_embed[0]).reshape(2, 6, 24, D)
    norm_a, norm_b, resid = call(
        norm_kernel,
        [shape(576, D), shape(576, D), shape(1152, D, dtype=F32)],
        [SMEM, VMEM, VMEM, VMEM],
        name="norm",
    )(flags, grid, embed, gain_attn[None])

    remote_b = send(norm_b, swap_b)
    remote_a = send(norm_a, swap_a)
    fwd_up = send(far_up, swap_core)
    fwd_down = send(far_down, swap_core)

    places = jnp.asarray(position_tables())
    places = jnp.where(parity == 1, places[1], places[0])
    onehot = (places[:, None] == jnp.arange(256, dtype=jnp.int32)[None, :]).astype(BF)
    query, key, value, wkv, wo, bias_in, bias_edge = call(
        qkv_kernel,
        [shape(2, 8, 72, D)] * 3
        + [shape(D, 1024), shape(D, D)]
        + [shape(2, 2, 576, 144, dtype=F32), shape(2, 2, 576, 288, dtype=F32)],
        [SMEM] + [VMEM] * 10,
        [pltpu.VMEM((D, D), BF), pltpu.VMEM((256, 256), BF), pltpu.VMEM((256, 256), BF)],
        name="qkv",
    )(
        flags, norm_a, norm_b, pack, mate, far_up, far_down, fwd_up, fwd_down,
        onehot[:432], onehot[432:],
    )

    weights = [pltpu.VMEM((D, 2048), BF), pltpu.VMEM((2048, D), BF), pltpu.SemaphoreType.DMA((2,))]

    def whole(array):
        return pl.BlockSpec(array.shape, lambda i: (0,) * array.ndim)

    def of_half(array, half):
        rank = array.ndim
        return pl.BlockSpec((1,) + array.shape[1:], lambda i: (half,) + (0,) * (rank - 1))

    def run_half(half, remote):
        outs = [shape(432, D, dtype=F32), shape(2, 72, D), shape(2, 72, D)]
        return pl.pallas_call(
            half_kernel,
            grid=(1,),
            out_shape=outs,
            in_specs=[
                whole(remote), of_half(query, half), of_half(key, half), of_half(value, half),
                whole(wkv), whole(wo), of_half(bias_in, half),
                pl.BlockSpec((576, D), lambda i: (half, 0)),
                pl.BlockSpec((1, D), lambda i: (0, 0)), ANY, ANY,
            ],
            out_specs=[whole(o) for o in outs],
            scratch_shapes=[
                pltpu.VMEM((6, 144, D), BF), pltpu.VMEM((6, 144, D), BF), pltpu.VMEM((432, D), F32),
            ] + weights,
            compiler_params=pltpu.CompilerParams(vmem_limit_bytes=48 * MIB),
            name="half_" + "ab"[half],
        )(remote, query, key, value, wkv, wo, bias_in, resid, gain_mlp[None], up_weight, down_weight)

    def edges(top):
        at = 432 if top else 504
        pick = lambda array: array[at : at + 72]
        return jnp.concatenate((pick(norm_a), pick(norm_b), pick(remote_b)), axis=0)

    below = send(edges(False), to_next)
    above = send(edges(True), to_last)
    inner_b, key_b, value_b = run_half(1, remote_b)
    below_a = send(remote_a[504:576], to_next)
    above_a = send(remote_a[432:504], to_last)
    inner_a, key_a, value_a = run_half(0, remote_a)

    edge_blocks = lambda array: pl.BlockSpec((2, 2, 72, D), lambda i: (0, 3, 0, 0))
    resid_edges = resid.reshape(2, 576, D)
    out_shape = shape(4, 2, 6, 24, D)
    out = pl.pallas_call(
        edge_kernel,
        grid=(1,),
        out_shape=out_shape,
        in_specs=[
            SMEM, whole(below), whole(below_a), whole(above), whole(above_a),
            edge_blocks(query), edge_blocks(key), edge_blocks(value),
            whole(key_a), whole(value_a), whole(key_b), whole(value_b),
            whole(wkv), whole(wo), whole(bias_edge),
            pl.BlockSpec((2, 144, D), lambda i: (0, 3, 0)),
            pl.BlockSpec((1, D), lambda i: (0, 0)),
            whole(inner_a), whole(inner_b), ANY, ANY,
        ],
        out_specs=whole(out_shape),
        scratch_shapes=[
            pltpu.VMEM((2, 4, 72, 1024), F32), pltpu.VMEM((288, D), BF), pltpu.VMEM((288, D), BF),
            pltpu.VMEM((288, D), F32), pltpu.VMEM((288, D), F32), pltpu.VMEM((4, 6, 24, D), F32),
        ] + weights,
        compiler_params=pltpu.CompilerParams(vmem_limit_bytes=56 * MIB),
        name="edge",
    )(
        flags, below, below_a, above, above_a, query, key, value, key_a, value_a, key_b, value_b,
        wkv, wo, bias_edge, resid_edges, gain_mlp[None], inner_a, inner_b, up_weight, down_weight,
    )
    return out.reshape(4, 12, 24, D).transpose(0, 2, 1, 3)


def solution(mesh):
    in_specs = (
        P(None, "head", "tile", None),
        P("head", "tile"),
        P(),
        P(),
        P(None, None, "head"),
        P("head", None),
        P("head", None, None),
        P("head", None, None),
        P(),
        P(),
        P(),
    )
    out_specs = P(None, "head", "tile", None)
    return jax.shard_map(shards, mesh=mesh, in_specs=in_specs, out_specs=out_specs, check_vma=False)
```

```python
import functools

import jax
import jax.numpy as jnp
import numpy as np
from jax import lax
from jax.experimental import pallas as pl
from jax.experimental.pallas import tpu as pltpu
from jax.sharding import PartitionSpec as P

D = 512
AXES = ("tile", "head")
BF = jnp.bfloat16
F32 = jnp.float32
MIB = 2**20
PLACE = {1: (0, 0), 2: (0, 1), 3: (1, 0), 0: (1, 1)}
NT = (((1,), (1,)), ((), ()))
PENALTY = -1000000000.0
VMEM = pl.BlockSpec(memory_space=pltpu.VMEM)
SMEM = pl.BlockSpec(memory_space=pltpu.SMEM)
ANY = pl.BlockSpec(memory_space=pl.ANY)
HBM = pl.BlockSpec(memory_space=pltpu.HBM)


def dot(left, right):
    return jnp.dot(left, right, preferred_element_type=F32)


def dot_nt(left, right):
    return lax.dot_general(left, right, NT, preferred_element_type=F32)


def layer_norm(values, norm_gain):
    average = jnp.mean(values, axis=-1, keepdims=True)
    centred = values - average
    variance = jnp.mean(centred * centred, axis=-1, keepdims=True)
    return centred * lax.rsqrt(variance + 1e-05) * norm_gain


def front_kernel(
    wqkv, wo, left, right, tokens_in, land_in, embed_in, gain_in, gain_mlp_in,
    up_out, down_out, whole_out, norm_b_out, norm_a_out, resid_b_out, resid_a_out, gain_mlp_out,
    whole, factors, tokens, land, embed, gain, gain_mlp, norm, resid, sems,
):
    parity = lax.rem(lax.axis_index("tile"), 2)
    copies = []

    def copy(source, target):
        copies.append(pltpu.make_async_copy(source, target, sems.at[len(copies)]))
        copies[-1].start()
        return copies[-1]

    small = [
        copy(*pair) for pair in (
            (land_in, land), (embed_in, embed), (gain_in, gain), (gain_mlp_in, gain_mlp),
            (left, factors.at[0]), (right, factors.at[1]),
        )
    ]
    packed = [copy(wqkv, whole.at[:1536])]
    for block in range(4):
        lanes = pl.ds(128 * block, 128)
        packed.append(copy(wo.at[:, lanes], whole.at[pl.ds(1536 + 128 * block, 128)]))
    loads = [copy(tokens_in.at[:, 1 - parity], tokens.at[1]), copy(tokens_in.at[:, parity], tokens.at[0])]
    for one in small:
        one.wait()
    for index in range(2):
        base = 2048 + 128 * index
        whole[base : base + 64, :] = factors[index, :, :128]
        whole[base + 64 : base + 128, :] = jnp.concatenate(
            (factors[index, :, 128:], jnp.zeros((64, 112), BF)), axis=1
        )
    for one in packed:
        one.wait()
    stores = [
        copy(whole.at[:1152], up_out), copy(whole.at[1152:], down_out), copy(whole, whole_out),
        copy(gain_mlp, gain_mlp_out),
    ]
    eye = lax.broadcasted_iota(jnp.int32, (24, 24), 0) == lax.broadcasted_iota(jnp.int32, (24, 24), 1)
    columns = dot_nt(eye.astype(F32), land[...].astype(F32))
    sea_row, land_row = embed[0:1, :], embed[1:2, :]
    for half in (1, 0):
        side = parity if half == 0 else 1 - parity
        mine = jnp.where(side == 0, columns[:, :6], columns[:, 6:])
        loads[1 - half].wait()
        for col in range(6):
            added = jnp.where(mine[:, col : col + 1] > 0.5, land_row, sea_row)
            for level in range(4):
                pair, inner = PLACE[level]
                row = tokens[half, level, col].astype(F32) + added
                for k in range(3):
                    at = (pair * 3 + k) * 72 + inner * 36 + col * 6
                    resid[half, at : at + 6, :] = row[3 + 6 * k : 9 + 6 * k, :]
                at = 432 + pair * 40 + inner * 18 + col * 3
                resid[half, at : at + 3, :] = row[:3, :]
                resid[half, at + 80 : at + 83, :] = row[21:, :]
        for at in (468, 508, 548, 588):
            resid[half, at : at + 4, :] = jnp.zeros((4, D), F32)
        stores.append(copy(resid.at[half], (resid_a_out, resid_b_out)[half]))
        for start, count in ((0, 144), (144, 144), (288, 144), (432, 160)):
            rows = slice(start, start + count)
            norm[half, rows, :] = layer_norm(resid[half, rows, :], gain[...]).astype(BF)
        stores.append(copy(norm.at[half], (norm_a_out, norm_b_out)[half]))
    for one in stores:
        one.wait()


def block_rows(block):
    return (72 * block, 72) if block < 6 else (432 + 80 * (block - 6), 80)


def repeat4(value):
    return jnp.concatenate((value,) * 4, axis=0)


def head_stack(value, width):
    lane = lax.broadcasted_iota(jnp.int32, value.shape, 1) // width
    return jnp.concatenate(
        [jnp.where(lane == head, value, 0.0) for head in range(4)], axis=0
    ).astype(BF)


def head_pick(stacked):
    count = stacked.shape[0] // 4
    lane = lax.broadcasted_iota(jnp.int32, (count, stacked.shape[1]), 1) // 64
    total = stacked[:count]
    for head in range(1, 4):
        total = jnp.where(lane == head, stacked[count * head : count * head + count], total)
    return total


def qkv_kernel(
    group, norm_a, norm_b, pos_query, pos_key, *refs
):
    parts = refs[: 2 * (1 + group)]
    query, key, value, wkv, wo, bias_in, bias_edge, wq, left, right = refs[2 * (1 + group) :]

    def part(source, row, count):
        if group == 0:
            return parts[source][row : row + count, :]
        first, second = parts[2 * source : 2 * source + 2]
        if row + count <= 1152:
            return first[row : row + count, :]
        return second[row - 1152 : row - 1152 + count, :]

    for source in range(2):
        lanes = slice(128 * source, 128 * source + 128)
        wq[:, lanes] = part(source, 0, 512)
        wkv[:, lanes] = part(source, 512, 512)
        more = slice(256 + 128 * source, 384 + 128 * source)
        wkv[:128, more] = part(source, 1024, 128)
        wkv[128:, more] = part(source, 1152, 384)
        for block in range(4):
            wo[lanes, 128 * block : 128 * block + 128] = part(source, 1536 + 128 * block, 128)
        rows = slice(64 * source, 64 * source + 64)
        left[rows, :128] = part(source, 2048, 64)
        left[rows, 128:] = part(source, 2112, 64)
        right[rows, :128] = part(source, 2176, 64)
        right[rows, 128:] = part(source, 2240, 64)
    for half, norm in enumerate((norm_a, norm_b)):
        got_q = dot(norm[...], wq[...]) * 0.125
        got_kv = dot(norm[...], wkv[...])
        for block in range(8):
            at, count = block_rows(block)
            query[half, block, :count] = got_q[at : at + count].astype(BF)
            key[half, block, :count] = got_kv[at : at + count, :256].astype(BF)
            value[half, block, :count] = got_kv[at : at + count, 256:].astype(BF)
    factors = dot_nt(pos_query[...], left[...])
    q_level = lax.broadcasted_iota(jnp.int32, (72, 144), 0) >= 36
    k_level = lax.rem(lax.broadcasted_iota(jnp.int32, (72, 144), 1), 72) >= 36
    split = repeat4(jnp.where(q_level == k_level, 0.0, PENALTY))
    row = lax.broadcasted_iota(jnp.int32, (40, 160), 0)
    lane = lax.broadcasted_iota(jnp.int32, (40, 160), 1)
    slot = lax.rem(lane, 40)
    halo = lax.rem(lane // 40, 2) == 1
    head = lax.axis_index("head")
    for half in range(2):
        own_rows = head_stack(factors[72 * half : 72 * half + 72, :], 32)
        keys = dot_nt(right[...], pos_key[144 * half : 144 * half + 144, :]).astype(BF)
        bias = dot(own_rows, keys)
        bias_in[half, 0] = bias
        bias_in[half, 1] = bias + split
        for side in range(2):
            at = 144 + 80 * half + 40 * (1 - side)
            own_rows = head_stack(factors[at : at + 40, :], 32)
            at = 288 + 320 * half + 160 * side
            keys = dot_nt(right[...], pos_key[at : at + 160, :]).astype(BF)
            bias = dot(own_rows, keys)
            outside = jnp.logical_and(halo, head == 3 * side)
            hidden = jnp.logical_or(slot >= 36, outside)
            bias_edge[half, side, 0] = bias + repeat4(jnp.where(hidden, PENALTY, 0.0))
            hidden = jnp.logical_or(hidden, (row >= 18) != (slot >= 18))
            bias_edge[half, side, 1] = bias + repeat4(jnp.where(hidden, PENALTY, 0.0))


def attend(query, keys, values, bias):
    scores = dot_nt(head_stack(query, 64), keys) + bias[...]
    weights = jnp.exp(scores - jnp.max(scores, axis=-1, keepdims=True))
    scale = 1.0 / jnp.sum(weights, axis=-1, keepdims=True)
    return head_pick(dot(weights.astype(BF), values) * scale)


def fetch_kernel(up_in, down_in, after, up, down, sems):
    copies = (
        pltpu.make_async_copy(up_in, up, sems.at[0]),
        pltpu.make_async_copy(down_in, down, sems.at[1]),
    )
    for one in copies:
        one.start()
    for one in copies:
        one.wait()


def feed_forward(heads, resid, wo_0, wo_1, gain, up, down, hidden):
    mixed = resid + dot(heads[0].astype(BF), wo_0[...]) + dot(heads[1].astype(BF), wo_1[...])
    second = layer_norm(mixed, gain[...]).astype(BF)
    for start in range(0, 2048, 512):
        inner = dot(second, up[:, start : start + 512])
        inner = 0.5 * inner * (1.0 + lax.erf(inner * 0.7071067811865476))
        hidden[:, start : start + 512] = inner.astype(BF)
    return mixed + dot(hidden[...], down[...])


def half_kernel(half, remote, resid, gain, up, down, *refs):
    groups = (refs[:6], refs[6:12])
    out, edge_key, edge_value, keys, values, heads, hidden = refs[12:]
    for group, (query, key, value, wkv, wo, bias) in enumerate(groups):
        got = dot(remote[...], wkv[...])
        for lanes, near, target, edge in ((0, key, keys, edge_key), (256, value, values, edge_value)):
            for block in range(8):
                at, count = block_rows(block)
                part = got[at : at + count, lanes : lanes + 256]
                if block < 6:
                    joined = jnp.concatenate((near[half, block, :72].astype(F32), part), axis=0)
                    target[block] = joined.astype(BF)
                else:
                    edge[group, block - 6] = part.astype(BF)
        for block in range(6):
            heads[group, 72 * block : 72 * block + 72, :] = attend(
                query[half, block, :72].astype(F32), keys[block], values[block], bias.at[half, block // 3]
            )
    out[...] = feed_forward(
        heads, resid[:432, :], groups[0][4], groups[1][4], gain, up, down, hidden
    )


def gather_kernel(after, remote_b, norm_b, norm_a, remote_a, first, second):
    odd = lax.rem(lax.axis_index("head"), 2) == 1
    for index, block in enumerate((norm_a, norm_b, remote_b, remote_a)):
        rows = slice(80 * index, 80 * index + 80)
        top, bottom = block[432:512, :], block[512:592, :]
        first[rows, :] = jnp.where(odd, top, bottom)
        second[rows, :] = jnp.where(odd, bottom, top)


def edge_kernel(
    first, second, key_a, value_a, key_b, value_b, resid_a, resid_b, gain, out_a, out_b, up, down, *refs
):
    groups = (refs[:6], refs[6:12])
    out, halo, heads, edges, grid, stage, hidden, sems = refs[12:]
    parity = lax.rem(lax.axis_index("tile"), 2)
    odd = lax.rem(lax.axis_index("head"), 2)
    for group, (query, key, value, wkv, wo, bias) in enumerate(groups):
        halo[1 - odd] = dot(first[...], wkv[...])
        halo[odd] = dot(second[...], wkv[...])
        for half in range(2):
            remote = ((key_a, value_a), (key_b, value_b))[half]
            near, far = ((0, 240), (80, 160))[half]
            for side in range(2):
                own_query = query[half, 6 + side].astype(F32)
                own = [ref[half, 6 + side].astype(F32) for ref in (key, value)]
                other = [ref[group, side].astype(F32) for ref in remote]
                for pair in range(2):
                    rows = slice(40 * pair, 40 * pair + 40)
                    joined = []
                    for index in range(2):
                        lanes = slice(256 * index, 256 * index + 256)
                        parts = (
                            own[index][rows], halo[side, near + 40 * pair : near + 40 * pair + 40, lanes],
                            other[index][rows], halo[side, far + 40 * pair : far + 40 * pair + 40, lanes],
                        )
                        joined.append(jnp.concatenate(parts, axis=0).astype(BF))
                    got = attend(own_query[rows], joined[0], joined[1], bias.at[half, side, pair])
                    at = 144 * half + 72 * side + 36 * pair
                    heads[group, at : at + 36, :] = got[:36]
    here = [r[at : at + 36, :] for r in (resid_a, resid_b) for at in (432, 472, 512, 552)]
    for index, part in enumerate(here):
        edges[36 * index : 36 * index + 36, :] = part
    edges[...] = feed_forward(
        heads, edges[...], groups[0][4], groups[1][4], gain, up, down, hidden
    )
    copies = []
    for half, inside in enumerate((out_a, out_b)):
        place = parity if half == 0 else 1 - parity
        for level in range(4):
            pair, inner = PLACE[level]
            for col in range(6):
                at = 144 * half + pair * 36 + inner * 18 + col * 3
                grid[level, col, :3, :] = edges[at : at + 3, :]
                grid[level, col, 21:, :] = edges[at + 72 : at + 75, :]
                for k in range(3):
                    at = (pair * 3 + k) * 72 + inner * 36 + col * 6
                    grid[level, col, 3 + 6 * k : 9 + 6 * k, :] = inside[at : at + 6, :]
                stage[half, level, col] = grid[level, col].astype(BF)
            copies.append(
                pltpu.make_async_copy(stage.at[half, level], out.at[level, place], sems.at[4 * half + level])
            )
            copies[-1].start()
    for one in copies:
        one.wait()


def call(kernel, out_shape, in_specs, scratch=(), limit=16, flops=0, out_specs=None, **extra):
    many = isinstance(out_shape, (list, tuple))
    return pl.pallas_call(
        kernel,
        out_shape=out_shape,
        in_specs=in_specs,
        out_specs=out_specs or ([VMEM] * len(out_shape) if many else VMEM),
        scratch_shapes=scratch,
        compiler_params=pltpu.CompilerParams(vmem_limit_bytes=limit * MIB),
        cost_estimate=pl.CostEstimate(flops=flops, bytes_accessed=2 * MIB, transcendentals=0),
        **extra,
    )


def shape(*dims, dtype=BF):
    return jax.ShapeDtypeStruct(dims, dtype)


def position_tables():
    tables = []
    for parity in range(2):
        columns = (1 - parity, parity)

        def inside(half):
            c = columns[half]
            return [l * 72 + r * 12 + 6 * c + col for l in range(2) for col in range(6) for r in range(6)]

        def edge(half, rows):
            c = columns[half]
            spots = [
                l * 72 + (3 * rows + r) * 12 + 6 * c + col
                for l in range(2) for col in range(6) for r in range(3)
            ]
            return spots + [-1] * 4

        query = inside(0) + inside(1)
        for half in range(2):
            query += edge(half, 0) + edge(half, 1)
        key = []
        for half in range(2):
            key += inside(half) + inside(1 - half)
        for half in range(2):
            for side in range(2):
                near = 1 - side
                for h in (half, 1 - half):
                    key += edge(h, near) + edge(h, 1 - near)
        tables.append(query + key)
    return np.array(tables, np.int32)


def pairs_of(tiles, move):
    pairs = []
    for tile in range(tiles):
        for head in range(4):
            target = move(tile, head)
            if target is not None:
                pairs.append((tile * 4 + head, (target[0] % tiles) * 4 + target[1]))
    return pairs


def shards(
    tokens, land_sea, land_embed, gain_attn, qkv_weight, out_weight, bias_left, bias_right,
    gain_mlp, up_weight, down_weight,
):
    tiles = lax.axis_size("tile")
    parity = lax.rem(lax.axis_index("tile"), 2)

    def along_y(steps):
        def move(t, h):
            high, rest = divmod(t, tiles // 2)
            y = (2 * high + h // 2 + steps) % 4
            return (y // 2) * (tiles // 2) + rest, (y % 2) * 2 + h % 2

        return move

    def send(value, move):
        return lax.ppermute(value, AXES, pairs_of(tiles, move))

    swap_a = lambda t, h: (t + 1 if t % 2 else t - 1, h)
    swap_b = lambda t, h: (t ^ 1, h)
    swap_core = lambda t, h: (t, h ^ 1)
    swap_chip = lambda t, h: (t, 3 - h) if h in (1, 2) else None

    grid = tokens.transpose(0, 2, 1, 3).reshape(4, 2, 6, 24, D)
    rows = [shape(592, D)] * 2 + [shape(592, D, dtype=F32)] * 2
    pack_up, pack_down, pack, norm_b, norm_a, resid_b, resid_a, gain_mlp = call(
        front_kernel,
        [shape(1152, 128), shape(1152, 128), shape(2304, 128)] + rows + [shape(1, D, dtype=F32)],
        [HBM] * 9,
        [
            pltpu.VMEM((2304, 128), BF), pltpu.VMEM((2, 64, 144), BF), pltpu.VMEM((2, 4, 6, 24, D), BF),
            pltpu.VMEM((12, 24), jnp.int32), pltpu.VMEM((2, D), F32), pltpu.VMEM((1, D), F32),
            pltpu.VMEM((1, D), F32), pltpu.VMEM((2, 592, D), BF), pltpu.VMEM((2, 592, D), F32),
            pltpu.SemaphoreType.DMA((21,)),
        ],
        limit=63,
        out_specs=[HBM] * 8,
        name="front",
    )(
        qkv_weight.reshape(1536, 128),
        out_weight,
        bias_left.transpose(0, 2, 1).reshape(64, 144),
        bias_right.transpose(0, 2, 1).reshape(64, 144),
        grid, land_sea.transpose(1, 0), land_embed, gain_attn[None], gain_mlp[None],
    )
    far_up = send(pack_up, along_y(1))
    far_down = send(pack_down, along_y(-1))
    mate = send(pack, swap_core)

    remote_b = send(norm_b, swap_b)
    remote_a = send(norm_a, swap_a)
    fwd_up = send(far_up, swap_core)
    fwd_down = send(far_down, swap_core)

    places = jnp.asarray(position_tables())
    places = jnp.where(parity == 1, places[1], places[0])
    onehot = (places[:, None] == jnp.arange(256, dtype=jnp.int32)[None, :]).astype(BF)
    def run_qkv(group, parts):
        return call(
            functools.partial(qkv_kernel, group),
            [shape(2, 8, 80, 256)] * 3
            + [shape(D, 512), shape(256, D)]
            + [shape(2, 2, 288, 144, dtype=F32), shape(2, 2, 2, 160, 160, dtype=F32)],
            [VMEM] * (4 + len(parts)),
            [pltpu.VMEM((D, 256), BF)] + [pltpu.VMEM((128, 256), BF)] * 2,
            flops=2 * 10**9,
            name="qkv_" + str(group),
        )(norm_a, norm_b, onehot[:304], onehot[304:], *parts)

    near = run_qkv(0, (pack, mate))
    up, down = call(
        fetch_kernel, [shape(D, 2048), shape(2048, D)], [HBM] * 3,
        [pltpu.SemaphoreType.DMA((2,))], flops=10**9, name="fetch",
    )(up_weight, down_weight, near[3])
    far = run_qkv(1, (far_up, far_down, fwd_up, fwd_down))
    heads = near[:6] + far[:6]

    def run_half(half, remote, resid):
        return call(
            functools.partial(half_kernel, half),
            [shape(432, D, dtype=F32), shape(2, 2, 80, 256), shape(2, 2, 80, 256)],
            [VMEM] * 17,
            [
                pltpu.VMEM((6, 144, 256), BF), pltpu.VMEM((6, 144, 256), BF),
                pltpu.VMEM((2, 432, 256), F32), pltpu.VMEM((432, 2048), BF),
            ],
            flops=4 * 10**9,
            name="half_" + "ab"[half],
        )(remote, resid, gain_mlp, up, down, *heads)

    inner_b, key_b, value_b = run_half(1, remote_b, resid_b)
    first, second = call(
        gather_kernel, [shape(320, D)] * 2, [ANY] + [VMEM] * 4, name="gather"
    )(key_b, remote_b, norm_b, norm_a, remote_a)
    first = send(first, swap_core)
    second = send(second, swap_chip)
    inner_a, key_a, value_a = run_half(0, remote_a, resid_a)

    out = call(
        edge_kernel,
        shape(4, 2, 6, 24, D),
        [VMEM] * 25,
        [
            pltpu.VMEM((2, 320, 512), F32), pltpu.VMEM((2, 288, 256), F32), pltpu.VMEM((288, D), F32),
            pltpu.VMEM((4, 6, 24, D), F32), pltpu.VMEM((2, 4, 6, 24, D), BF), pltpu.VMEM((288, 2048), BF),
            pltpu.SemaphoreType.DMA((8,)),
        ],
        out_specs=ANY,
        flops=4 * 10**9,
        name="edge",
    )(
        first, second, key_a, value_a, key_b, value_b, resid_a, resid_b, gain_mlp, inner_a, inner_b,
        up, down, *near[:5], near[6], *far[:5], far[6],
    )
    return out.reshape(4, 12, 24, D).transpose(0, 2, 1, 3)


def solution(mesh):
    in_specs = (
        P(None, "head", "tile", None),
        P("head", "tile"),
        P(),
        P(),
        P(None, None, "head"),
        P("head", None),
        P("head", None, None),
        P("head", None, None),
        P(),
        P(),
        P(),
    )
    out_specs = P(None, "head", "tile", None)
    return jax.shard_map(shards, mesh=mesh, in_specs=in_specs, out_specs=out_specs, check_vma=False)
```

```python
import functools

import jax
import jax.numpy as jnp
import numpy as np
from jax import lax
from jax.experimental import pallas as pl
from jax.experimental.pallas import tpu as pltpu
from jax.sharding import PartitionSpec as P

D = 512
AXES = ("tile", "head")
BF = jnp.bfloat16
F32 = jnp.float32
MIB = 2**20
PLACE = {1: (0, 0), 2: (0, 1), 3: (1, 0), 0: (1, 1)}
NT = (((1,), (1,)), ((), ()))
PENALTY = -1000000000.0
VMEM = pl.BlockSpec(memory_space=pltpu.VMEM)
SMEM = pl.BlockSpec(memory_space=pltpu.SMEM)
ANY = pl.BlockSpec(memory_space=pl.ANY)
HBM = pl.BlockSpec(memory_space=pltpu.HBM)


def dot(left, right):
    return jnp.dot(left, right, preferred_element_type=F32)


def dot_nt(left, right):
    return lax.dot_general(left, right, NT, preferred_element_type=F32)


def layer_norm(values, norm_gain):
    average = jnp.mean(values, axis=-1, keepdims=True)
    centred = values - average
    variance = jnp.mean(centred * centred, axis=-1, keepdims=True)
    return centred * lax.rsqrt(variance + 1e-05) * norm_gain


class Copies:
    def __init__(self, sems):
        self.sems, self.count = sems, 0

    def __call__(self, source, target):
        one = pltpu.make_async_copy(source, target, self.sems.at[self.count])
        one.start()
        self.count += 1
        return one


def wait_all(copies):
    for one in copies:
        one.wait()


def pack_kernel(wqkv, wo, left, right, out, whole, factors, sems):
    copy = Copies(sems)
    small = [copy(left, factors.at[0]), copy(right, factors.at[1])]
    loads = [copy(wqkv, whole.at[:1536])]
    for block in range(4):
        lanes = pl.ds(128 * block, 128)
        loads.append(copy(wo.at[:, lanes], whole.at[pl.ds(1536 + 128 * block, 128)]))
    wait_all(small)
    for index in range(2):
        base = 2048 + 128 * index
        whole[base : base + 64, :] = factors[index, :, :128]
        whole[base + 64 : base + 128, :] = jnp.concatenate(
            (factors[index, :, 128:], jnp.zeros((64, 112), BF)), axis=1
        )
    wait_all(loads)
    wait_all([copy(whole, out)])


def norm_kernel(
    tokens_in, land_in, embed_in, gain_in, gain_mlp_in, after,
    norm_b_out, norm_a_out, resid_b_out, resid_a_out, gain_mlp_out,
    tokens, land, embed, gain, gain_mlp, norm, resid, sems,
):
    parity = lax.rem(lax.axis_index("tile"), 2)
    copy = Copies(sems)
    small = [copy(land_in, land), copy(embed_in, embed), copy(gain_in, gain), copy(gain_mlp_in, gain_mlp)]
    loads = [copy(tokens_in.at[:, 1 - parity], tokens.at[1]), copy(tokens_in.at[:, parity], tokens.at[0])]
    wait_all(small)
    stores = [copy(gain_mlp, gain_mlp_out)]
    eye = lax.broadcasted_iota(jnp.int32, (24, 24), 0) == lax.broadcasted_iota(jnp.int32, (24, 24), 1)
    columns = dot_nt(eye.astype(F32), land[...].astype(F32))
    sea_row, land_row = embed[0:1, :], embed[1:2, :]
    for half in (1, 0):
        side = parity if half == 0 else 1 - parity
        mine = jnp.where(side == 0, columns[:, :6], columns[:, 6:])
        loads[1 - half].wait()
        for col in range(6):
            added = jnp.where(mine[:, col : col + 1] > 0.5, land_row, sea_row)
            for level in range(4):
                pair, inner = PLACE[level]
                row = tokens[half, level, col].astype(F32) + added
                for k in range(3):
                    at = (pair * 3 + k) * 72 + inner * 36 + col * 6
                    resid[half, at : at + 6, :] = row[3 + 6 * k : 9 + 6 * k, :]
                at = 432 + pair * 40 + inner * 18 + col * 3
                resid[half, at : at + 3, :] = row[:3, :]
                resid[half, at + 80 : at + 83, :] = row[21:, :]
        for at in (468, 508, 548, 588):
            resid[half, at : at + 4, :] = jnp.zeros((4, D), F32)
        stores.append(copy(resid.at[half], (resid_a_out, resid_b_out)[half]))
        for start, count in ((0, 144), (144, 144), (288, 144), (432, 160)):
            rows = slice(start, start + count)
            norm[half, rows, :] = layer_norm(resid[half, rows, :], gain[...]).astype(BF)
        stores.append(copy(norm.at[half], (norm_a_out, norm_b_out)[half]))
    wait_all(stores)


def block_rows(block):
    return (72 * block, 72) if block < 6 else (432 + 80 * (block - 6), 80)


def repeat4(value):
    return jnp.concatenate((value,) * 4, axis=0)


def head_stack(value, width):
    lane = lax.broadcasted_iota(jnp.int32, value.shape, 1) // width
    return jnp.concatenate(
        [jnp.where(lane == head, value, 0.0) for head in range(4)], axis=0
    ).astype(BF)


def head_pick(stacked):
    count = stacked.shape[0] // 4
    lane = lax.broadcasted_iota(jnp.int32, (count, stacked.shape[1]), 1) // 64
    total = stacked[:count]
    for head in range(1, 4):
        total = jnp.where(lane == head, stacked[count * head : count * head + count], total)
    return total


def qkv_kernel(group, norm_a, norm_b, pos_query, pos_key, *refs):
    parts, norms = refs[:2], (norm_a, norm_b)
    query, key, value, wkv, wo, bias_in, bias_edge = refs[2:9]
    wq, left, right = refs[-3:]
    def part(source, row, count):
        return parts[source][row : row + count, :]

    for source in range(2):
        lanes = slice(128 * source, 128 * source + 128)
        wq[:, lanes] = part(source, 0, 512)
        wkv[:, lanes] = part(source, 512, 512)
        more = slice(256 + 128 * source, 384 + 128 * source)
        wkv[:, more] = part(source, 1024, 512)
        for block in range(4):
            wo[lanes, 128 * block : 128 * block + 128] = part(source, 1536 + 128 * block, 128)
        rows = slice(64 * source, 64 * source + 64)
        left[rows, :128] = part(source, 2048, 64)
        left[rows, 128:] = part(source, 2112, 64)
        right[rows, :128] = part(source, 2176, 64)
        right[rows, 128:] = part(source, 2240, 64)
    factors = dot_nt(pos_query[...], left[...])
    q_level = lax.broadcasted_iota(jnp.int32, (72, 144), 0) >= 36
    k_level = lax.rem(lax.broadcasted_iota(jnp.int32, (72, 144), 1), 72) >= 36
    split = repeat4(jnp.where(q_level == k_level, 0.0, PENALTY))
    row = lax.broadcasted_iota(jnp.int32, (40, 160), 0)
    lane = lax.broadcasted_iota(jnp.int32, (40, 160), 1)
    slot = lax.rem(lane, 40)
    halo = lax.rem(lane // 40, 2) == 1
    head = lax.axis_index("head")
    for half in range(2):
        own_rows = head_stack(factors[72 * half : 72 * half + 72, :], 32)
        keys = dot_nt(right[...], pos_key[144 * half : 144 * half + 144, :]).astype(BF)
        bias = dot(own_rows, keys)
        bias_in[half, 0] = bias
        bias_in[half, 1] = bias + split
        for side in range(2):
            at = 144 + 80 * half + 40 * (1 - side)
            own_rows = head_stack(factors[at : at + 40, :], 32)
            at = 288 + 320 * half + 160 * side
            keys = dot_nt(right[...], pos_key[at : at + 160, :]).astype(BF)
            bias = dot(own_rows, keys)
            outside = jnp.logical_and(halo, head == 3 * side)
            hidden = jnp.logical_or(slot >= 36, outside)
            bias_edge[half, side, 0] = bias + repeat4(jnp.where(hidden, PENALTY, 0.0))
            hidden = jnp.logical_or(hidden, (row >= 18) != (slot >= 18))
            bias_edge[half, side, 1] = bias + repeat4(jnp.where(hidden, PENALTY, 0.0))
    for half, norm in enumerate(norms):
        got_q = dot(norm[...], wq[...]) * 0.125
        got_kv = dot(norm[...], wkv[...])
        for block in range(8):
            at, count = block_rows(block)
            query[half, block, :count] = got_q[at : at + count].astype(BF)
            key[half, block, :count] = got_kv[at : at + count, :256].astype(BF)
            value[half, block, :count] = got_kv[at : at + count, 256:].astype(BF)


def attend(query, keys, values, bias):
    scores = dot_nt(head_stack(query, 64), keys) + bias[...]
    weights = jnp.exp(scores - jnp.max(scores, axis=-1, keepdims=True))
    scale = 1.0 / jnp.sum(weights, axis=-1, keepdims=True)
    return head_pick(dot(weights.astype(BF), values) * scale)


def fetch_kernel(up_in, down_in, after, up, down, sems):
    copies = (
        pltpu.make_async_copy(up_in, up, sems.at[0]),
        pltpu.make_async_copy(down_in, down, sems.at[1]),
    )
    for one in copies:
        one.start()
    for one in copies:
        one.wait()


def feed_forward(heads, resid, wo_0, wo_1, gain, up, down, hidden):
    mixed = resid + dot(heads[0].astype(BF), wo_0[...]) + dot(heads[1].astype(BF), wo_1[...])
    second = layer_norm(mixed, gain[...]).astype(BF)
    for start in range(0, 2048, 512):
        inner = dot(second, up[:, start : start + 512])
        inner = 0.5 * inner * (1.0 + lax.erf(inner * 0.7071067811865476))
        hidden[:, start : start + 512] = inner.astype(BF)
    return mixed + dot(hidden[...], down[...])


def half_kernel(half, remote, resid, gain, up, down, *refs):
    groups = (refs[:6], refs[6:12])
    out, edge_key, edge_value, keys, values, heads, hidden, inside = refs[12:]
    for group, (query, key, value, wkv, wo, bias) in enumerate(groups):
        got = dot(remote[...], wkv[...])
        for lanes, near, target, edge in ((0, key, keys, edge_key), (256, value, values, edge_value)):
            for block in range(8):
                at, count = block_rows(block)
                part = got[at : at + count, lanes : lanes + 256]
                if block < 6:
                    joined = jnp.concatenate((near[half, block, :72].astype(F32), part), axis=0)
                    target[block] = joined.astype(BF)
                else:
                    edge[group, block - 6] = part.astype(BF)
        for block in range(6):
            heads[group, 72 * block : 72 * block + 72, :] = attend(
                query[half, block, :72].astype(F32), keys[block], values[block], bias.at[half, block // 3]
            )
    inside[...] = feed_forward(
        heads, resid[:432, :], groups[0][4], groups[1][4], gain, up, down, hidden
    )
    for level in range(4):
        pair, inner = PLACE[level]
        for col in range(6):
            for k in range(3):
                at = (pair * 3 + k) * 72 + inner * 36 + col * 6
                out[level, col, 3 + 6 * k : 9 + 6 * k, :] = inside[at : at + 6, :]
            out[level, col, :3, :] = jnp.zeros((3, D), F32)
            out[level, col, 21:, :] = jnp.zeros((3, D), F32)


def gather_kernel(count, *refs):
    blocks, (first, second) = refs[:count], refs[-2:]
    odd = lax.rem(lax.axis_index("head"), 2) == 1
    for index, block in enumerate(blocks):
        rows = slice(80 * index, 80 * index + 80)
        top, bottom = block[432:512, :], block[512:592, :]
        first[rows, :] = jnp.where(odd, top, bottom)
        second[rows, :] = jnp.where(odd, bottom, top)


def edge_kernel(
    first, second, key_a, value_a, key_b, value_b, resid_a, resid_b, gain,
    out_a, out_b, up, down, *refs
):
    groups = (refs[:6], refs[6:12])
    out, halo, heads, edges, stage, hidden, sems = refs[12:]
    parity = lax.rem(lax.axis_index("tile"), 2)
    odd = lax.rem(lax.axis_index("head"), 2)
    for group, (query, key, value, wkv, wo, bias) in enumerate(groups):
        halo[1 - odd] = dot(first[...], wkv[...])
        halo[odd] = dot(second[...], wkv[...])
        for half in range(2):
            remote = ((key_a, value_a), (key_b, value_b))[half]
            near, far = ((160, 240), (0, 80))[half]
            for side in range(2):
                own_query = query[half, 6 + side].astype(F32)
                own = [ref[half, 6 + side].astype(F32) for ref in (key, value)]
                other = [ref[group, side].astype(F32) for ref in remote]
                for pair in range(2):
                    rows = slice(40 * pair, 40 * pair + 40)
                    joined = []
                    for index in range(2):
                        lanes = slice(256 * index, 256 * index + 256)
                        parts = (
                            own[index][rows], halo[side, near + 40 * pair : near + 40 * pair + 40, lanes],
                            other[index][rows], halo[side, far + 40 * pair : far + 40 * pair + 40, lanes],
                        )
                        joined.append(jnp.concatenate(parts, axis=0).astype(BF))
                    got = attend(own_query[rows], joined[0], joined[1], bias.at[half, side, pair])
                    at = 144 * half + 72 * side + 36 * pair
                    heads[group, at : at + 36, :] = got[:36]
    here = [r[at : at + 36, :] for r in (resid_a, resid_b) for at in (432, 472, 512, 552)]
    for index, part in enumerate(here):
        edges[36 * index : 36 * index + 36, :] = part
    edges[...] = feed_forward(
        heads, edges[...], groups[0][4], groups[1][4], gain, up, down, hidden
    )
    copies = []
    for half, inside in enumerate((out_a, out_b)):
        place = parity if half == 0 else 1 - parity
        for level in range(4):
            pair, inner = PLACE[level]
            for col in range(6):
                at = 144 * half + pair * 36 + inner * 18 + col * 3
                whole = (edges[at : at + 3, :], inside[level, col, 3:21, :], edges[at + 72 : at + 75, :])
                stage[half, level, col] = jnp.concatenate(whole, axis=0).astype(BF)
            copies.append(
                pltpu.make_async_copy(stage.at[half, level], out.at[level, place], sems.at[4 * half + level])
            )
            copies[-1].start()
    for one in copies:
        one.wait()


def call(kernel, out_shape, in_specs, scratch=(), limit=16, flops=0, out_specs=None, **extra):
    many = isinstance(out_shape, (list, tuple))
    return pl.pallas_call(
        kernel,
        out_shape=out_shape,
        in_specs=in_specs,
        out_specs=out_specs or ([VMEM] * len(out_shape) if many else VMEM),
        scratch_shapes=scratch,
        compiler_params=pltpu.CompilerParams(vmem_limit_bytes=limit * MIB),
        cost_estimate=pl.CostEstimate(flops=flops, bytes_accessed=2 * MIB, transcendentals=0),
        **extra,
    )


def shape(*dims, dtype=BF):
    return jax.ShapeDtypeStruct(dims, dtype)


def position_tables():
    tables = []
    for parity in range(2):
        columns = (1 - parity, parity)

        def inside(half):
            c = columns[half]
            return [l * 72 + r * 12 + 6 * c + col for l in range(2) for col in range(6) for r in range(6)]

        def edge(half, rows):
            c = columns[half]
            spots = [
                l * 72 + (3 * rows + r) * 12 + 6 * c + col
                for l in range(2) for col in range(6) for r in range(3)
            ]
            return spots + [-1] * 4

        query = inside(0) + inside(1)
        for half in range(2):
            query += edge(half, 0) + edge(half, 1)
        key = []
        for half in range(2):
            key += inside(half) + inside(1 - half)
        for half in range(2):
            for side in range(2):
                near = 1 - side
                for h in (half, 1 - half):
                    key += edge(h, near) + edge(h, 1 - near)
        tables.append(query + key)
    return np.array(tables, np.int32)


def pairs_of(tiles, move):
    pairs = []
    for tile in range(tiles):
        for head in range(4):
            target = move(tile, head)
            if target is not None:
                pairs.append((tile * 4 + head, (target[0] % tiles) * 4 + target[1]))
    return pairs


def shards(
    tokens, land_sea, land_embed, gain_attn, qkv_weight, out_weight, bias_left, bias_right,
    gain_mlp, up_weight, down_weight,
):
    tiles = lax.axis_size("tile")
    parity = lax.rem(lax.axis_index("tile"), 2)

    def along_y(t, h):
        high, rest = divmod(t, tiles // 2)
        y = (2 * high + h // 2 + (-1 if h % 2 else 1)) % 4
        return (y // 2) * (tiles // 2) + rest, (y % 2) * 2 + h % 2

    def send(value, move):
        return lax.ppermute(value, AXES, pairs_of(tiles, move))

    swap_a = lambda t, h: (t + 1 if t % 2 else t - 1, h)
    swap_b = lambda t, h: (t ^ 1, h)
    swap_core = lambda t, h: (t, h ^ 1)
    swap_chip = lambda t, h: (t, 3 - h) if h in (1, 2) else None

    pack = call(
        pack_kernel,
        shape(2304, 128),
        [HBM] * 4,
        [pltpu.VMEM((2304, 128), BF), pltpu.VMEM((2, 64, 144), BF), pltpu.SemaphoreType.DMA((8,))],
        limit=63,
        out_specs=HBM,
        name="pack",
    )(
        qkv_weight.reshape(1536, 128),
        out_weight,
        bias_left.transpose(0, 2, 1).reshape(64, 144),
        bias_right.transpose(0, 2, 1).reshape(64, 144),
    )
    far = send(pack, along_y)

    grid = tokens.transpose(0, 2, 1, 3).reshape(4, 2, 6, 24, D)
    rows = [shape(592, D)] * 2 + [shape(592, D, dtype=F32)] * 2
    norm_b, norm_a, resid_b, resid_a, gain_mlp = call(
        norm_kernel,
        rows + [shape(1, D, dtype=F32)],
        [HBM] * 6,
        [
            pltpu.VMEM((2, 4, 6, 24, D), BF), pltpu.VMEM((12, 24), jnp.int32), pltpu.VMEM((2, D), F32),
            pltpu.VMEM((1, D), F32), pltpu.VMEM((1, D), F32), pltpu.VMEM((2, 592, D), BF),
            pltpu.VMEM((2, 592, D), F32), pltpu.SemaphoreType.DMA((11,)),
        ],
        limit=63,
        out_specs=[HBM] * 5,
        name="norm",
    )(grid, land_sea.transpose(1, 0), land_embed, gain_attn[None], gain_mlp[None], pack)

    remote_b = send(norm_b, swap_b)
    remote_a = send(norm_a, swap_a)
    own, far = lax.optimization_barrier((pack, far))
    mate = send(own, swap_core)
    forwarded = send(far, swap_core)

    places = jnp.asarray(position_tables())
    places = jnp.where(parity == 1, places[1], places[0])
    onehot = (places[:, None] == jnp.arange(256, dtype=jnp.int32)[None, :]).astype(BF)
    def run_qkv(group, norms, parts):
        return call(
            functools.partial(qkv_kernel, group),
            [shape(2, 8, 80, 256)] * 3
            + [shape(D, 512), shape(256, D)]
            + [shape(2, 2, 288, 144, dtype=F32), shape(2, 2, 2, 160, 160, dtype=F32)],
            [VMEM] * 6,
            [pltpu.VMEM((D, 256), BF)] + [pltpu.VMEM((128, 256), BF)] * 2,
            flops=2 * 10**9,
            name="qkv_" + str(group),
        )(*norms, onehot[:304], onehot[304:], *parts)

    near = run_qkv(0, (norm_a, norm_b), (own, far))
    up, down = call(
        fetch_kernel, [shape(D, 2048), shape(2048, D)], [HBM] * 3,
        [pltpu.SemaphoreType.DMA((2,))], flops=10**9, name="fetch",
    )(up_weight, down_weight, near[3])
    rest = run_qkv(1, (norm_a, norm_b), (mate, forwarded))
    heads = near[:6] + rest[:6]

    def run_half(half, remote, resid):
        return call(
            functools.partial(half_kernel, half),
            [shape(4, 6, 24, D, dtype=F32), shape(2, 2, 80, 256), shape(2, 2, 80, 256)],
            [VMEM] * 17,
            [
                pltpu.VMEM((6, 144, 256), BF), pltpu.VMEM((6, 144, 256), BF),
                pltpu.VMEM((2, 432, 256), F32), pltpu.VMEM((432, 2048), BF),
                pltpu.VMEM((432, D), F32),
            ],
            flops=4 * 10**9,
            name="half_" + "ab"[half],
        )(remote, resid, gain_mlp, up, down, *heads)

    inner_b, key_b, value_b = run_half(1, remote_b, resid_b)
    def run_gather(blocks, after, name):
        first, second = call(
            functools.partial(gather_kernel, len(blocks)),
            [shape(80 * len(blocks), D)] * 2, [VMEM] * len(blocks) + [ANY], name=name,
        )(*blocks, after)
        return send(first, swap_core), send(second, swap_chip)

    first, second = run_gather((norm_b, remote_b, norm_a, remote_a), key_b, "gather")
    inner_a, key_a, value_a = run_half(0, remote_a, resid_a)

    out = call(
        edge_kernel,
        shape(4, 2, 6, 24, D),
        [VMEM] * 25,
        [
            pltpu.VMEM((2, 320, 512), F32), pltpu.VMEM((2, 288, 256), F32), pltpu.VMEM((288, D), F32),
            pltpu.VMEM((2, 4, 6, 24, D), BF), pltpu.VMEM((288, 2048), BF),
            pltpu.SemaphoreType.DMA((8,)),
        ],
        out_specs=ANY,
        flops=4 * 10**9,
        name="edge",
    )(
        first, second, key_a, value_a, key_b, value_b, resid_a, resid_b, gain_mlp, inner_a, inner_b,
        up, down, *near[:5], near[6], *rest[:5], rest[6],
    )
    return out.reshape(4, 12, 24, D).transpose(0, 2, 1, 3)


def solution(mesh):
    in_specs = (
        P(None, "head", "tile", None),
        P("head", "tile"),
        P(),
        P(),
        P(None, None, "head"),
        P("head", None),
        P("head", None, None),
        P("head", None, None),
        P(),
        P(),
        P(),
    )
    out_specs = P(None, "head", "tile", None)
    return jax.shard_map(shards, mesh=mesh, in_specs=in_specs, out_specs=out_specs, check_vma=False)
```

```python
import functools

import jax
import jax.numpy as jnp
import numpy as np
from jax import lax
from jax.experimental import pallas as pl
from jax.experimental.pallas import tpu as pltpu
from jax.sharding import PartitionSpec as P

D = 512
AXES = ("tile", "head")
BF = jnp.bfloat16
F32 = jnp.float32
MIB = 2**20
PLACE = {1: (0, 0), 2: (0, 1), 3: (1, 0), 0: (1, 1)}
NT = (((1,), (1,)), ((), ()))
PENALTY = -1000000000.0
VMEM = pl.BlockSpec(memory_space=pltpu.VMEM)
SMEM = pl.BlockSpec(memory_space=pltpu.SMEM)
ANY = pl.BlockSpec(memory_space=pl.ANY)
HBM = pl.BlockSpec(memory_space=pltpu.HBM)


def dot(left, right):
    return jnp.dot(left, right, preferred_element_type=F32)


def dot_nt(left, right):
    return lax.dot_general(left, right, NT, preferred_element_type=F32)


def layer_norm(values, norm_gain):
    average = jnp.mean(values, axis=-1, keepdims=True)
    centred = values - average
    variance = jnp.mean(centred * centred, axis=-1, keepdims=True)
    return centred * lax.rsqrt(variance + 1e-05) * norm_gain


class Copies:
    def __init__(self, sems):
        self.sems, self.count = sems, 0

    def __call__(self, source, target):
        one = pltpu.make_async_copy(source, target, self.sems.at[self.count])
        one.start()
        self.count += 1
        return one


def wait_all(copies):
    for one in copies:
        one.wait()


def pack_kernel(wqkv, wo, left, right, out, whole, factors, sems):
    copy = Copies(sems)
    small = [copy(left, factors.at[0]), copy(right, factors.at[1])]
    loads = [copy(wqkv, whole.at[:1536])]
    for block in range(4):
        lanes = pl.ds(128 * block, 128)
        loads.append(copy(wo.at[:, lanes], whole.at[pl.ds(1536 + 128 * block, 128)]))
    wait_all(small)
    for index in range(2):
        base = 2048 + 128 * index
        whole[base : base + 64, :] = factors[index, :, :128]
        whole[base + 64 : base + 128, :] = jnp.concatenate(
            (factors[index, :, 128:], jnp.zeros((64, 112), BF)), axis=1
        )
    wait_all(loads)
    wait_all([copy(whole, out)])


def norm_kernel(
    tokens_in, land_in, embed_in, gain_in, gain_mlp_in, after,
    norm_b_out, norm_a_out, resid_b_out, resid_a_out, gain_mlp_out,
    tokens, land, embed, gain, gain_mlp, norm, resid, sems,
):
    parity = lax.rem(lax.axis_index("tile"), 2)
    copy = Copies(sems)
    small = [copy(land_in, land), copy(embed_in, embed), copy(gain_in, gain), copy(gain_mlp_in, gain_mlp)]
    loads = [copy(tokens_in.at[:, 1 - parity], tokens.at[1]), copy(tokens_in.at[:, parity], tokens.at[0])]
    wait_all(small)
    stores = [copy(gain_mlp, gain_mlp_out)]
    eye = lax.broadcasted_iota(jnp.int32, (24, 24), 0) == lax.broadcasted_iota(jnp.int32, (24, 24), 1)
    columns = dot_nt(eye.astype(F32), land[...].astype(F32))
    sea_row, land_row = embed[0:1, :], embed[1:2, :]
    for half in (1, 0):
        side = parity if half == 0 else 1 - parity
        mine = jnp.where(side == 0, columns[:, :6], columns[:, 6:])
        loads[1 - half].wait()
        for col in range(6):
            added = jnp.where(mine[:, col : col + 1] > 0.5, land_row, sea_row)
            for level in range(4):
                pair, inner = PLACE[level]
                row = tokens[half, level, col].astype(F32) + added
                for k in range(3):
                    at = (pair * 3 + k) * 72 + inner * 36 + col * 6
                    resid[half, at : at + 6, :] = row[3 + 6 * k : 9 + 6 * k, :]
                at = 432 + pair * 40 + inner * 18 + col * 3
                resid[half, at : at + 3, :] = row[:3, :]
                resid[half, at + 80 : at + 83, :] = row[21:, :]
        for at in (468, 508, 548, 588):
            resid[half, at : at + 4, :] = jnp.zeros((4, D), F32)
        stores.append(copy(resid.at[half], (resid_a_out, resid_b_out)[half]))
        for start, count in ((0, 144), (144, 144), (288, 144), (432, 160)):
            rows = slice(start, start + count)
            norm[half, rows, :] = layer_norm(resid[half, rows, :], gain[...]).astype(BF)
        stores.append(copy(norm.at[half], (norm_a_out, norm_b_out)[half]))
    wait_all(stores)


def block_rows(block):
    return (72 * block, 72) if block < 6 else (432 + 80 * (block - 6), 80)


def repeat4(value):
    return jnp.concatenate((value,) * 4, axis=0)


def head_stack(value, width):
    lane = lax.broadcasted_iota(jnp.int32, value.shape, 1) // width
    return jnp.concatenate(
        [jnp.where(lane == head, value, 0.0) for head in range(4)], axis=0
    ).astype(BF)


def head_pick(stacked):
    count = stacked.shape[0] // 4
    lane = lax.broadcasted_iota(jnp.int32, (count, stacked.shape[1]), 1) // 64
    total = stacked[:count]
    for head in range(1, 4):
        total = jnp.where(lane == head, stacked[count * head : count * head + count], total)
    return total


def qkv_kernel(group, norm_a, norm_b, pos_query, pos_key, *refs):
    parts, norms = refs[:2], (norm_a, norm_b)
    query, key, value, wkv, wo, bias_in, bias_edge = refs[2:9]
    wq, left, right = refs[-3:]
    def part(source, row, count):
        return parts[source][row : row + count, :]

    for source in range(2):
        lanes = slice(128 * source, 128 * source + 128)
        wq[:, lanes] = part(source, 0, 512)
        wkv[:, lanes] = part(source, 512, 512)
        more = slice(256 + 128 * source, 384 + 128 * source)
        wkv[:, more] = part(source, 1024, 512)
        for block in range(4):
            wo[lanes, 128 * block : 128 * block + 128] = part(source, 1536 + 128 * block, 128)
        rows = slice(64 * source, 64 * source + 64)
        left[rows, :128] = part(source, 2048, 64)
        left[rows, 128:] = part(source, 2112, 64)
        right[rows, :128] = part(source, 2176, 64)
        right[rows, 128:] = part(source, 2240, 64)
    factors = dot_nt(pos_query[...], left[...])
    q_level = lax.broadcasted_iota(jnp.int32, (72, 144), 0) >= 36
    k_level = lax.rem(lax.broadcasted_iota(jnp.int32, (72, 144), 1), 72) >= 36
    split = repeat4(jnp.where(q_level == k_level, 0.0, PENALTY))
    row = lax.broadcasted_iota(jnp.int32, (40, 160), 0)
    lane = lax.broadcasted_iota(jnp.int32, (40, 160), 1)
    slot = lax.rem(lane, 40)
    halo = lax.rem(lane // 40, 2) == 1
    head = lax.axis_index("head")
    for half in range(2):
        own_rows = head_stack(factors[72 * half : 72 * half + 72, :], 32)
        keys = dot_nt(right[...], pos_key[144 * half : 144 * half + 144, :]).astype(BF)
        bias = dot(own_rows, keys)
        bias_in[half, 0] = bias
        bias_in[half, 1] = bias + split
        for side in range(2):
            at = 144 + 80 * half + 40 * (1 - side)
            own_rows = head_stack(factors[at : at + 40, :], 32)
            at = 288 + 320 * half + 160 * side
            keys = dot_nt(right[...], pos_key[at : at + 160, :]).astype(BF)
            bias = dot(own_rows, keys)
            outside = jnp.logical_and(halo, head == 3 * side)
            hidden = jnp.logical_or(slot >= 36, outside)
            bias_edge[half, side, 0] = bias + repeat4(jnp.where(hidden, PENALTY, 0.0))
            hidden = jnp.logical_or(hidden, (row >= 18) != (slot >= 18))
            bias_edge[half, side, 1] = bias + repeat4(jnp.where(hidden, PENALTY, 0.0))
    for half, norm in enumerate(norms):
        got_q = dot(norm[...], wq[...]) * 0.125
        got_kv = dot(norm[...], wkv[...])
        for block in range(8):
            at, count = block_rows(block)
            query[half, block, :count] = got_q[at : at + count].astype(BF)
            key[half, block, :count] = got_kv[at : at + count, :256].astype(BF)
            value[half, block, :count] = got_kv[at : at + count, 256:].astype(BF)


def attend(query, keys, values, bias):
    scores = dot_nt(head_stack(query, 64), keys) + bias[...]
    weights = jnp.exp(scores - jnp.max(scores, axis=-1, keepdims=True))
    scale = 1.0 / jnp.sum(weights, axis=-1, keepdims=True)
    return head_pick(dot(weights.astype(BF), values) * scale)


def fetch_kernel(up_in, down_in, after, up, down, sems):
    copies = (
        pltpu.make_async_copy(up_in, up, sems.at[0]),
        pltpu.make_async_copy(down_in, down, sems.at[1]),
    )
    for one in copies:
        one.start()
    for one in copies:
        one.wait()


def feed_forward(heads, resid, wo_0, wo_1, gain, up, down, hidden):
    mixed = resid + dot(heads[0].astype(BF), wo_0[...]) + dot(heads[1].astype(BF), wo_1[...])
    second = layer_norm(mixed, gain[...]).astype(BF)
    for start in range(0, 2048, 512):
        inner = dot(second, up[:, start : start + 512])
        inner = 0.5 * inner * (1.0 + lax.erf(inner * 0.7071067811865476))
        hidden[:, start : start + 512] = inner.astype(BF)
    return mixed + dot(hidden[...], down[...])


def half_kernel(half, remote, resid, gain, up, down, *refs):
    groups = (refs[:6], refs[6:12])
    out, edge_key, edge_value, keys, values, heads, hidden, inside = refs[12:]
    for group, (query, key, value, wkv, wo, bias) in enumerate(groups):
        got = dot(remote[...], wkv[...])
        for lanes, near, target, edge in ((0, key, keys, edge_key), (256, value, values, edge_value)):
            for block in range(8):
                at, count = block_rows(block)
                part = got[at : at + count, lanes : lanes + 256]
                if block < 6:
                    joined = jnp.concatenate((near[half, block, :72].astype(F32), part), axis=0)
                    target[block] = joined.astype(BF)
                else:
                    edge[group, block - 6] = part.astype(BF)
        for block in range(6):
            heads[group, 72 * block : 72 * block + 72, :] = attend(
                query[half, block, :72].astype(F32), keys[block], values[block], bias.at[half, block // 3]
            )
    inside[...] = feed_forward(
        heads, resid[:432, :], groups[0][4], groups[1][4], gain, up, down, hidden
    )
    for level in range(4):
        pair, inner = PLACE[level]
        for col in range(6):
            for k in range(3):
                at = (pair * 3 + k) * 72 + inner * 36 + col * 6
                out[level, col, 3 + 6 * k : 9 + 6 * k, :] = inside[at : at + 6, :]
            out[level, col, :3, :] = jnp.zeros((3, D), F32)
            out[level, col, 21:, :] = jnp.zeros((3, D), F32)


def gather_kernel(count, *refs):
    blocks, (first, second) = refs[:count], refs[-2:]
    odd = lax.rem(lax.axis_index("head"), 2) == 1
    for index, block in enumerate(blocks):
        rows = slice(80 * index, 80 * index + 80)
        top, bottom = block[432:512, :], block[512:592, :]
        first[rows, :] = jnp.where(odd, top, bottom)
        second[rows, :] = jnp.where(odd, bottom, top)


def side_of(which):
    odd = lax.rem(lax.axis_index("head"), 2)
    return odd if which else 1 - odd


def edge_attend(which, exchange, remotes, groups, halo, heads):
    side = side_of(which)
    for group, (query, key, value, wkv, wo, bias) in enumerate(groups):
        halo[...] = dot(exchange[...], wkv[...])
        for half in range(2):
            near, far = ((160, 240), (0, 80))[half]
            own_query = query[half, 6 + side].astype(F32)
            own = [ref[half, 6 + side].astype(F32) for ref in (key, value)]
            other = [ref[group, side].astype(F32) for ref in remotes[half]]
            for pair in range(2):
                rows = slice(40 * pair, 40 * pair + 40)
                joined = []
                for index in range(2):
                    lanes = slice(256 * index, 256 * index + 256)
                    parts = (
                        own[index][rows], halo[near + 40 * pair : near + 40 * pair + 40, lanes],
                        other[index][rows], halo[far + 40 * pair : far + 40 * pair + 40, lanes],
                    )
                    joined.append(jnp.concatenate(parts, axis=0).astype(BF))
                got = attend(own_query[rows], joined[0], joined[1], bias.at[half, side, pair])
                at = 144 * which + 72 * half + 36 * pair
                heads[group, at : at + 36, :] = got[:36]


def first_edge_kernel(first, key_a, value_a, key_b, value_b, *refs):
    groups, (heads, halo) = (refs[:6], refs[6:12]), refs[12:]
    edge_attend(0, first, ((key_a, value_a), (key_b, value_b)), groups, halo, heads)


def edge_kernel(
    second, key_a, value_a, key_b, value_b, before, resid_a, resid_b, gain, out_a, out_b, up, down, *refs
):
    groups = (refs[:6], refs[6:12])
    out, halo, heads, resid, edges, stage, hidden, sems = refs[12:]
    parity = lax.rem(lax.axis_index("tile"), 2)
    heads[:, :144, :] = before[...]
    edge_attend(1, second, ((key_a, value_a), (key_b, value_b)), groups, halo, heads)
    for which in range(2):
        for half, source in enumerate((resid_a, resid_b)):
            for pair in range(2):
                start = pl.multiple_of(432 + 80 * side_of(which) + 40 * pair, 8)
                at = 144 * which + 72 * half + 36 * pair
                resid[at : at + 36, :] = source[pl.ds(start, 40), :][:36]
    done = feed_forward(heads, resid[...], groups[0][4], groups[1][4], gain, up, down, hidden)
    edges[0] = done[:144]
    edges[1] = done[144:]
    odd = lax.rem(lax.axis_index("head"), 2)
    copies = []
    for half, inside in enumerate((out_a, out_b)):
        place = parity if half == 0 else 1 - parity
        for level in range(4):
            pair, inner = PLACE[level]
            for col in range(6):
                at = 72 * half + pair * 36 + inner * 18 + col * 3
                whole = (
                    edges[1 - odd, at : at + 3, :], inside[level, col, 3:21, :], edges[odd, at : at + 3, :]
                )
                stage[half, level, col] = jnp.concatenate(whole, axis=0).astype(BF)
            copies.append(
                pltpu.make_async_copy(stage.at[half, level], out.at[level, place], sems.at[4 * half + level])
            )
            copies[-1].start()
    wait_all(copies)


def call(kernel, out_shape, in_specs, scratch=(), limit=16, flops=0, out_specs=None, **extra):
    many = isinstance(out_shape, (list, tuple))
    return pl.pallas_call(
        kernel,
        out_shape=out_shape,
        in_specs=in_specs,
        out_specs=out_specs or ([VMEM] * len(out_shape) if many else VMEM),
        scratch_shapes=scratch,
        compiler_params=pltpu.CompilerParams(vmem_limit_bytes=limit * MIB),
        cost_estimate=pl.CostEstimate(flops=flops, bytes_accessed=2 * MIB, transcendentals=0),
        **extra,
    )


def shape(*dims, dtype=BF):
    return jax.ShapeDtypeStruct(dims, dtype)


def position_tables():
    tables = []
    for parity in range(2):
        columns = (1 - parity, parity)

        def inside(half):
            c = columns[half]
            return [l * 72 + r * 12 + 6 * c + col for l in range(2) for col in range(6) for r in range(6)]

        def edge(half, rows):
            c = columns[half]
            spots = [
                l * 72 + (3 * rows + r) * 12 + 6 * c + col
                for l in range(2) for col in range(6) for r in range(3)
            ]
            return spots + [-1] * 4

        query = inside(0) + inside(1)
        for half in range(2):
            query += edge(half, 0) + edge(half, 1)
        key = []
        for half in range(2):
            key += inside(half) + inside(1 - half)
        for half in range(2):
            for side in range(2):
                near = 1 - side
                for h in (half, 1 - half):
                    key += edge(h, near) + edge(h, 1 - near)
        tables.append(query + key)
    return np.array(tables, np.int32)


def pairs_of(tiles, move):
    pairs = []
    for tile in range(tiles):
        for head in range(4):
            target = move(tile, head)
            if target is not None:
                pairs.append((tile * 4 + head, (target[0] % tiles) * 4 + target[1]))
    return pairs


def shards(
    tokens, land_sea, land_embed, gain_attn, qkv_weight, out_weight, bias_left, bias_right,
    gain_mlp, up_weight, down_weight,
):
    tiles = lax.axis_size("tile")
    parity = lax.rem(lax.axis_index("tile"), 2)

    def along_y(t, h):
        high, rest = divmod(t, tiles // 2)
        y = (2 * high + h // 2 + (-1 if h % 2 else 1)) % 4
        return (y // 2) * (tiles // 2) + rest, (y % 2) * 2 + h % 2

    def send(value, move):
        return lax.ppermute(value, AXES, pairs_of(tiles, move))

    swap_a = lambda t, h: (t + 1 if t % 2 else t - 1, h)
    swap_b = lambda t, h: (t ^ 1, h)
    swap_core = lambda t, h: (t, h ^ 1)
    swap_chip = lambda t, h: (t, 3 - h) if h in (1, 2) else None

    pack = call(
        pack_kernel,
        shape(2304, 128),
        [HBM] * 4,
        [pltpu.VMEM((2304, 128), BF), pltpu.VMEM((2, 64, 144), BF), pltpu.SemaphoreType.DMA((8,))],
        limit=63,
        out_specs=HBM,
        name="pack",
    )(
        qkv_weight.reshape(1536, 128),
        out_weight,
        bias_left.transpose(0, 2, 1).reshape(64, 144),
        bias_right.transpose(0, 2, 1).reshape(64, 144),
    )
    far = send(pack, along_y)

    grid = tokens.transpose(0, 2, 1, 3).reshape(4, 2, 6, 24, D)
    rows = [shape(592, D)] * 2 + [shape(592, D, dtype=F32)] * 2
    norm_b, norm_a, resid_b, resid_a, gain_mlp = call(
        norm_kernel,
        rows + [shape(1, D, dtype=F32)],
        [HBM] * 6,
        [
            pltpu.VMEM((2, 4, 6, 24, D), BF), pltpu.VMEM((12, 24), jnp.int32), pltpu.VMEM((2, D), F32),
            pltpu.VMEM((1, D), F32), pltpu.VMEM((1, D), F32), pltpu.VMEM((2, 592, D), BF),
            pltpu.VMEM((2, 592, D), F32), pltpu.SemaphoreType.DMA((11,)),
        ],
        limit=63,
        out_specs=[HBM] * 5,
        name="norm",
    )(grid, land_sea.transpose(1, 0), land_embed, gain_attn[None], gain_mlp[None], pack)

    remote_b = send(norm_b, swap_b)
    remote_a = send(norm_a, swap_a)
    own, far = lax.optimization_barrier((pack, far))
    mate = send(own, swap_core)
    forwarded = send(far, swap_core)

    places = jnp.asarray(position_tables())
    places = jnp.where(parity == 1, places[1], places[0])
    onehot = (places[:, None] == jnp.arange(256, dtype=jnp.int32)[None, :]).astype(BF)
    def run_qkv(group, norms, parts):
        return call(
            functools.partial(qkv_kernel, group),
            [shape(2, 8, 80, 256)] * 3
            + [shape(D, 512), shape(256, D)]
            + [shape(2, 2, 288, 144, dtype=F32), shape(2, 2, 2, 160, 160, dtype=F32)],
            [VMEM] * 6,
            [pltpu.VMEM((D, 256), BF)] + [pltpu.VMEM((128, 256), BF)] * 2,
            flops=2 * 10**9,
            name="qkv_" + str(group),
        )(*norms, onehot[:304], onehot[304:], *parts)

    near = run_qkv(0, (norm_a, norm_b), (own, far))
    up, down = call(
        fetch_kernel, [shape(D, 2048), shape(2048, D)], [HBM] * 3,
        [pltpu.SemaphoreType.DMA((2,))], flops=10**9, name="fetch",
    )(up_weight, down_weight, near[3])
    rest = run_qkv(1, (norm_a, norm_b), (mate, forwarded))
    heads = near[:6] + rest[:6]

    def run_half(half, remote, resid):
        return call(
            functools.partial(half_kernel, half),
            [shape(4, 6, 24, D, dtype=F32), shape(2, 2, 80, 256), shape(2, 2, 80, 256)],
            [VMEM] * 17,
            [
                pltpu.VMEM((6, 144, 256), BF), pltpu.VMEM((6, 144, 256), BF),
                pltpu.VMEM((2, 432, 256), F32), pltpu.VMEM((432, 2048), BF),
                pltpu.VMEM((432, D), F32),
            ],
            flops=4 * 10**9,
            name="half_" + "ab"[half],
        )(remote, resid, gain_mlp, up, down, *heads)

    inner_b, key_b, value_b = run_half(1, remote_b, resid_b)
    def run_gather(blocks, after, name):
        first, second = call(
            functools.partial(gather_kernel, len(blocks)),
            [shape(80 * len(blocks), D)] * 2, [VMEM] * len(blocks) + [ANY], name=name,
        )(*blocks, after)
        return send(first, swap_core), send(second, swap_chip)

    first, second = run_gather((norm_b, remote_b, norm_a, remote_a), key_b, "gather")
    inner_a, key_a, value_a = run_half(0, remote_a, resid_a)

    remotes = (key_a, value_a, key_b, value_b)
    edge_heads = (*near[:5], near[6], *rest[:5], rest[6])
    before = call(
        first_edge_kernel,
        shape(2, 144, 256, dtype=F32),
        [VMEM] * 17,
        [pltpu.VMEM((320, 512), F32)],
        flops=10**9,
        name="edge_first",
    )(first, *remotes, *edge_heads)
    out = call(
        edge_kernel,
        shape(4, 2, 6, 24, D),
        [VMEM] * 25,
        [
            pltpu.VMEM((320, 512), F32), pltpu.VMEM((2, 288, 256), F32), pltpu.VMEM((288, D), F32),
            pltpu.VMEM((2, 144, D), F32), pltpu.VMEM((2, 4, 6, 24, D), BF), pltpu.VMEM((288, 2048), BF),
            pltpu.SemaphoreType.DMA((8,)),
        ],
        out_specs=ANY,
        flops=4 * 10**9,
        name="edge",
    )(second, *remotes, before, resid_a, resid_b, gain_mlp, inner_a, inner_b, up, down, *edge_heads)
    return out.reshape(4, 12, 24, D).transpose(0, 2, 1, 3)


def solution(mesh):
    in_specs = (
        P(None, "head", "tile", None),
        P("head", "tile"),
        P(),
        P(),
        P(None, None, "head"),
        P("head", None),
        P("head", None, None),
        P("head", None, None),
        P(),
        P(),
        P(),
    )
    out_specs = P(None, "head", "tile", None)
    return jax.shard_map(shards, mesh=mesh, in_specs=in_specs, out_specs=out_specs, check_vma=False)
```

```python
import functools

import jax
import jax.numpy as jnp
import numpy as np
from jax import lax
from jax.experimental import pallas as pl
from jax.experimental.pallas import tpu as pltpu
from jax.sharding import PartitionSpec as P

D = 512
AXES = ("tile", "head")
BF = jnp.bfloat16
F32 = jnp.float32
MIB = 2**20
PLACE = {1: (0, 0), 2: (0, 1), 3: (1, 0), 0: (1, 1)}
NT = (((1,), (1,)), ((), ()))
PENALTY = -1000000000.0
VMEM = pl.BlockSpec(memory_space=pltpu.VMEM)
SMEM = pl.BlockSpec(memory_space=pltpu.SMEM)
ANY = pl.BlockSpec(memory_space=pl.ANY)
HBM = pl.BlockSpec(memory_space=pltpu.HBM)


def dot(left, right):
    return jnp.dot(left, right, preferred_element_type=F32)


def dot_nt(left, right):
    return lax.dot_general(left, right, NT, preferred_element_type=F32)


def layer_norm(values, norm_gain):
    average = jnp.mean(values, axis=-1, keepdims=True)
    centred = values - average
    variance = jnp.mean(centred * centred, axis=-1, keepdims=True)
    return centred * lax.rsqrt(variance + 1e-05) * norm_gain


class Copies:
    def __init__(self, sems):
        self.sems, self.count = sems, 0

    def __call__(self, source, target):
        one = pltpu.make_async_copy(source, target, self.sems.at[self.count])
        one.start()
        self.count += 1
        return one


def wait_all(copies):
    for one in copies:
        one.wait()


def pack_kernel(wqkv, wo, left, right, out, whole, factors, sems):
    copy = Copies(sems)
    small = [copy(left, factors.at[0]), copy(right, factors.at[1])]
    loads = [copy(wqkv, whole.at[:1536])]
    for block in range(4):
        lanes = pl.ds(128 * block, 128)
        loads.append(copy(wo.at[:, lanes], whole.at[pl.ds(1536 + 128 * block, 128)]))
    wait_all(small)
    for index in range(2):
        base = 2048 + 128 * index
        whole[base : base + 64, :] = factors[index, :, :128]
        whole[base + 64 : base + 128, :] = jnp.concatenate(
            (factors[index, :, 128:], jnp.zeros((64, 112), BF)), axis=1
        )
    wait_all(loads)
    wait_all([copy(whole, out)])


def norm_kernel(
    tokens_in, land_in, embed_in, gain_in, gain_mlp_in, after,
    norm_b_out, norm_a_out, resid_b_out, resid_a_out, gain_mlp_out,
    tokens, land, embed, gain, gain_mlp, norm, resid, sems,
):
    parity = lax.rem(lax.axis_index("tile"), 2)
    copy = Copies(sems)
    small = [copy(land_in, land), copy(embed_in, embed), copy(gain_in, gain), copy(gain_mlp_in, gain_mlp)]
    loads = [copy(tokens_in.at[:, 1 - parity], tokens.at[1]), copy(tokens_in.at[:, parity], tokens.at[0])]
    wait_all(small)
    stores = [copy(gain_mlp, gain_mlp_out)]
    eye = lax.broadcasted_iota(jnp.int32, (24, 24), 0) == lax.broadcasted_iota(jnp.int32, (24, 24), 1)
    columns = dot_nt(eye.astype(F32), land[...].astype(F32))
    sea_row, land_row = embed[0:1, :], embed[1:2, :]
    for half in (1, 0):
        side = parity if half == 0 else 1 - parity
        mine = jnp.where(side == 0, columns[:, :6], columns[:, 6:])
        loads[1 - half].wait()
        for col in range(6):
            added = jnp.where(mine[:, col : col + 1] > 0.5, land_row, sea_row)
            for level in range(4):
                pair, inner = PLACE[level]
                row = tokens[half, level, col].astype(F32) + added
                for k in range(3):
                    at = (pair * 3 + k) * 72 + inner * 36 + col * 6
                    resid[half, at : at + 6, :] = row[3 + 6 * k : 9 + 6 * k, :]
                at = 432 + pair * 40 + inner * 18 + col * 3
                resid[half, at : at + 3, :] = row[:3, :]
                resid[half, at + 80 : at + 83, :] = row[21:, :]
        for at in (468, 508, 548, 588):
            resid[half, at : at + 4, :] = jnp.zeros((4, D), F32)
        stores.append(copy(resid.at[half], (resid_a_out, resid_b_out)[half]))
        for start, count in ((0, 144), (144, 144), (288, 144), (432, 160)):
            rows = slice(start, start + count)
            norm[half, rows, :] = layer_norm(resid[half, rows, :], gain[...]).astype(BF)
        stores.append(copy(norm.at[half], (norm_a_out, norm_b_out)[half]))
    wait_all(stores)


def block_rows(block):
    return (72 * block, 72) if block < 6 else (432 + 80 * (block - 6), 80)


def repeat4(value):
    return jnp.concatenate((value,) * 4, axis=0)


def head_stack(value, width):
    lane = lax.broadcasted_iota(jnp.int32, value.shape, 1) // width
    return jnp.concatenate(
        [jnp.where(lane == head, value, 0.0) for head in range(4)], axis=0
    ).astype(BF)


def head_pick(stacked):
    count = stacked.shape[0] // 4
    lane = lax.broadcasted_iota(jnp.int32, (count, stacked.shape[1]), 1) // 64
    total = stacked[:count]
    for head in range(1, 4):
        total = jnp.where(lane == head, stacked[count * head : count * head + count], total)
    return total


def qkv_kernel(group, norm_a, norm_b, pos_query, pos_key, after, *refs):
    parts, norms = refs[:2], (norm_a, norm_b)
    query, key, value, wkv, wo, bias_in, bias_edge = refs[2:9]
    wq, left, right = refs[-3:]
    def part(source, row, count):
        return parts[source][row : row + count, :]

    for source in range(2):
        lanes = slice(128 * source, 128 * source + 128)
        wq[:, lanes] = part(source, 0, 512)
        wkv[:, lanes] = part(source, 512, 512)
        more = slice(256 + 128 * source, 384 + 128 * source)
        wkv[:, more] = part(source, 1024, 512)
        for block in range(4):
            wo[lanes, 128 * block : 128 * block + 128] = part(source, 1536 + 128 * block, 128)
        rows = slice(64 * source, 64 * source + 64)
        left[rows, :128] = part(source, 2048, 64)
        left[rows, 128:] = part(source, 2112, 64)
        right[rows, :128] = part(source, 2176, 64)
        right[rows, 128:] = part(source, 2240, 64)
    factors = dot_nt(pos_query[...], left[...])
    q_level = lax.broadcasted_iota(jnp.int32, (72, 144), 0) >= 36
    k_level = lax.rem(lax.broadcasted_iota(jnp.int32, (72, 144), 1), 72) >= 36
    split = repeat4(jnp.where(q_level == k_level, 0.0, PENALTY))
    row = lax.broadcasted_iota(jnp.int32, (40, 160), 0)
    lane = lax.broadcasted_iota(jnp.int32, (40, 160), 1)
    slot = lax.rem(lane, 40)
    halo = lax.rem(lane // 40, 2) == 1
    head = lax.axis_index("head")
    for half in range(2):
        own_rows = head_stack(factors[72 * half : 72 * half + 72, :], 32)
        keys = dot_nt(right[...], pos_key[144 * half : 144 * half + 144, :]).astype(BF)
        bias = dot(own_rows, keys)
        bias_in[half, 0] = bias
        bias_in[half, 1] = bias + split
        for side in range(2):
            at = 144 + 80 * half + 40 * (1 - side)
            own_rows = head_stack(factors[at : at + 40, :], 32)
            at = 288 + 320 * half + 160 * side
            keys = dot_nt(right[...], pos_key[at : at + 160, :]).astype(BF)
            bias = dot(own_rows, keys)
            outside = jnp.logical_and(halo, head == 3 * side)
            hidden = jnp.logical_or(slot >= 36, outside)
            bias_edge[half, side, 0] = bias + repeat4(jnp.where(hidden, PENALTY, 0.0))
            hidden = jnp.logical_or(hidden, (row >= 18) != (slot >= 18))
            bias_edge[half, side, 1] = bias + repeat4(jnp.where(hidden, PENALTY, 0.0))
    for half, norm in enumerate(norms):
        got_q = dot(norm[...], wq[...]) * 0.125
        got_kv = dot(norm[...], wkv[...])
        for block in range(8):
            at, count = block_rows(block)
            query[half, block, :count] = got_q[at : at + count].astype(BF)
            key[half, block, :count] = got_kv[at : at + count, :256].astype(BF)
            value[half, block, :count] = got_kv[at : at + count, 256:].astype(BF)


def attend(query, keys, values, bias):
    scores = dot_nt(head_stack(query, 64), keys) + bias[...]
    weights = jnp.exp(scores - jnp.max(scores, axis=-1, keepdims=True))
    scale = 1.0 / jnp.sum(weights, axis=-1, keepdims=True)
    return head_pick(dot(weights.astype(BF), values) * scale)


def fetch_kernel(up_in, down_in, after, up, down, sems):
    copies = (
        pltpu.make_async_copy(up_in, up, sems.at[0]),
        pltpu.make_async_copy(down_in, down, sems.at[1]),
    )
    for one in copies:
        one.start()
    for one in copies:
        one.wait()


def feed_forward(heads, resid, wo_0, wo_1, gain, up, down, hidden):
    mixed = resid + dot(heads[0].astype(BF), wo_0[...]) + dot(heads[1].astype(BF), wo_1[...])
    second = layer_norm(mixed, gain[...]).astype(BF)
    for start in range(0, 2048, 512):
        inner = dot(second, up[:, start : start + 512])
        inner = 0.5 * inner * (1.0 + lax.erf(inner * 0.7071067811865476))
        hidden[:, start : start + 512] = inner.astype(BF)
    return mixed + dot(hidden[...], down[...])


def half_kernel(half, remote, resid, gain, up, down, *refs):
    groups = (refs[:6], refs[6:12])
    out, edge_key, edge_value, keys, values, heads, hidden, inside = refs[12:]
    for group, (query, key, value, wkv, wo, bias) in enumerate(groups):
        got = dot(remote[...], wkv[...])
        for lanes, near, target, edge in ((0, key, keys, edge_key), (256, value, values, edge_value)):
            for block in range(8):
                at, count = block_rows(block)
                part = got[at : at + count, lanes : lanes + 256]
                if block < 6:
                    joined = jnp.concatenate((near[half, block, :72].astype(F32), part), axis=0)
                    target[block] = joined.astype(BF)
                else:
                    edge[group, block - 6] = part.astype(BF)
        for block in range(6):
            heads[group, 72 * block : 72 * block + 72, :] = attend(
                query[half, block, :72].astype(F32), keys[block], values[block], bias.at[half, block // 3]
            )
    inside[...] = feed_forward(
        heads, resid[:432, :], groups[0][4], groups[1][4], gain, up, down, hidden
    )
    for level in range(4):
        pair, inner = PLACE[level]
        for col in range(6):
            for k in range(3):
                at = (pair * 3 + k) * 72 + inner * 36 + col * 6
                out[level, col, 3 + 6 * k : 9 + 6 * k, :] = inside[at : at + 6, :]


def gather_kernel(count, *refs):
    blocks, (first, second) = refs[:count], refs[-2:]
    odd = lax.rem(lax.axis_index("head"), 2) == 1
    for index, block in enumerate(blocks):
        rows = slice(80 * index, 80 * index + 80)
        top, bottom = block[432:512, :], block[512:592, :]
        first[rows, :] = jnp.where(odd, top, bottom)
        second[rows, :] = jnp.where(odd, bottom, top)


def side_of(which):
    odd = lax.rem(lax.axis_index("head"), 2)
    return odd if which else 1 - odd


def edge_attend(which, exchange, remotes, groups, halo, heads):
    side = side_of(which)
    for group, (query, key, value, wkv, wo, bias) in enumerate(groups):
        halo[...] = dot(exchange[...], wkv[...])
        for half in range(2):
            near, far = ((160, 240), (0, 80))[half]
            own_query = query[half, 6 + side].astype(F32)
            own = [ref[half, 6 + side].astype(F32) for ref in (key, value)]
            other = [ref[group, side].astype(F32) for ref in remotes[half]]
            for pair in range(2):
                rows = slice(40 * pair, 40 * pair + 40)
                joined = []
                for index in range(2):
                    lanes = slice(256 * index, 256 * index + 256)
                    parts = (
                        own[index][rows], halo[near + 40 * pair : near + 40 * pair + 40, lanes],
                        other[index][rows], halo[far + 40 * pair : far + 40 * pair + 40, lanes],
                    )
                    joined.append(jnp.concatenate(parts, axis=0).astype(BF))
                got = attend(own_query[rows], joined[0], joined[1], bias.at[half, side, pair])
                at = 144 * which + 72 * half + 36 * pair
                heads[group, at : at + 36, :] = got[:36]


def first_edge_kernel(first, key_a, value_a, key_b, value_b, *refs):
    groups, (heads, halo) = (refs[:6], refs[6:12]), refs[12:]
    edge_attend(0, first, ((key_a, value_a), (key_b, value_b)), groups, halo, heads)


def edge_kernel(
    second, key_a, value_a, key_b, value_b, before, resid_a, resid_b, gain, out_a, out_b, up, down, *refs
):
    groups = (refs[:6], refs[6:12])
    out, halo, heads, resid, edges, stage, hidden, sems = refs[12:]
    parity = lax.rem(lax.axis_index("tile"), 2)
    heads[:, :144, :] = before[...]
    edge_attend(1, second, ((key_a, value_a), (key_b, value_b)), groups, halo, heads)
    for which in range(2):
        for half, source in enumerate((resid_a, resid_b)):
            for pair in range(2):
                start = pl.multiple_of(432 + 80 * side_of(which) + 40 * pair, 8)
                at = 144 * which + 72 * half + 36 * pair
                resid[at : at + 36, :] = source[pl.ds(start, 40), :][:36]
    done = feed_forward(heads, resid[...], groups[0][4], groups[1][4], gain, up, down, hidden)
    edges[0] = done[:144]
    edges[1] = done[144:]
    odd = lax.rem(lax.axis_index("head"), 2)
    copies = []
    for half, inside in enumerate((out_a, out_b)):
        place = parity if half == 0 else 1 - parity
        for level in range(4):
            pair, inner = PLACE[level]
            for col in range(6):
                at = 72 * half + pair * 36 + inner * 18 + col * 3
                whole = (
                    edges[1 - odd, at : at + 3, :], inside[level, col, 3:21, :], edges[odd, at : at + 3, :]
                )
                stage[half, level, col] = jnp.concatenate(whole, axis=0).astype(BF)
            copies.append(
                pltpu.make_async_copy(stage.at[half, level], out.at[level, place], sems.at[4 * half + level])
            )
            copies[-1].start()
    wait_all(copies)


def tick_kernel(after, out):
    out[...] = jnp.zeros_like(out)


def call(kernel, out_shape, in_specs, scratch=(), limit=16, flops=0, out_specs=None, **extra):
    many = isinstance(out_shape, (list, tuple))
    return pl.pallas_call(
        kernel,
        out_shape=out_shape,
        in_specs=in_specs,
        out_specs=out_specs or ([VMEM] * len(out_shape) if many else VMEM),
        scratch_shapes=scratch,
        compiler_params=pltpu.CompilerParams(vmem_limit_bytes=limit * MIB),
        cost_estimate=pl.CostEstimate(flops=flops, bytes_accessed=2 * MIB, transcendentals=0),
        **extra,
    )


def shape(*dims, dtype=BF):
    return jax.ShapeDtypeStruct(dims, dtype)


def position_tables():
    tables = []
    for parity in range(2):
        columns = (1 - parity, parity)

        def inside(half):
            c = columns[half]
            return [l * 72 + r * 12 + 6 * c + col for l in range(2) for col in range(6) for r in range(6)]

        def edge(half, rows):
            c = columns[half]
            spots = [
                l * 72 + (3 * rows + r) * 12 + 6 * c + col
                for l in range(2) for col in range(6) for r in range(3)
            ]
            return spots + [-1] * 4

        query = inside(0) + inside(1)
        for half in range(2):
            query += edge(half, 0) + edge(half, 1)
        key = []
        for half in range(2):
            key += inside(half) + inside(1 - half)
        for half in range(2):
            for side in range(2):
                near = 1 - side
                for h in (half, 1 - half):
                    key += edge(h, near) + edge(h, 1 - near)
        tables.append(query + key)
    return np.array(tables, np.int32)


def pairs_of(tiles, move):
    pairs = []
    for tile in range(tiles):
        for head in range(4):
            target = move(tile, head)
            if target is not None:
                pairs.append((tile * 4 + head, (target[0] % tiles) * 4 + target[1]))
    return pairs


def shards(
    tokens, land_sea, land_embed, gain_attn, qkv_weight, out_weight, bias_left, bias_right,
    gain_mlp, up_weight, down_weight,
):
    tiles = lax.axis_size("tile")
    parity = lax.rem(lax.axis_index("tile"), 2)

    def along_y(t, h):
        high, rest = divmod(t, tiles // 2)
        y = (2 * high + h // 2 + (-1 if h % 2 else 1)) % 4
        return (y // 2) * (tiles // 2) + rest, (y % 2) * 2 + h % 2

    def send(value, move):
        return lax.ppermute(value, AXES, pairs_of(tiles, move))

    swap_a = lambda t, h: (t + 1 if t % 2 else t - 1, h)
    swap_b = lambda t, h: (t ^ 1, h)
    swap_core = lambda t, h: (t, h ^ 1)
    swap_chip = lambda t, h: (t, 3 - h) if h in (1, 2) else None

    pack = call(
        pack_kernel,
        shape(2304, 128),
        [HBM] * 4,
        [pltpu.VMEM((2304, 128), BF), pltpu.VMEM((2, 64, 144), BF), pltpu.SemaphoreType.DMA((8,))],
        limit=63,
        out_specs=HBM,
        name="pack",
    )(
        qkv_weight.reshape(1536, 128),
        out_weight,
        bias_left.transpose(0, 2, 1).reshape(64, 144),
        bias_right.transpose(0, 2, 1).reshape(64, 144),
    )
    far = send(pack, along_y)

    grid = tokens.transpose(0, 2, 1, 3).reshape(4, 2, 6, 24, D)
    rows = [shape(592, D)] * 2 + [shape(592, D, dtype=F32)] * 2
    norm_b, norm_a, resid_b, resid_a, gain_mlp = call(
        norm_kernel,
        rows + [shape(1, D, dtype=F32)],
        [HBM] * 6,
        [
            pltpu.VMEM((2, 4, 6, 24, D), BF), pltpu.VMEM((12, 24), jnp.int32), pltpu.VMEM((2, D), F32),
            pltpu.VMEM((1, D), F32), pltpu.VMEM((1, D), F32), pltpu.VMEM((2, 592, D), BF),
            pltpu.VMEM((2, 592, D), F32), pltpu.SemaphoreType.DMA((11,)),
        ],
        limit=63,
        out_specs=[HBM] * 5,
        name="norm",
    )(grid, land_sea.transpose(1, 0), land_embed, gain_attn[None], gain_mlp[None], pack)

    remote_b = send(norm_b, swap_b)
    remote_a = send(norm_a, swap_a)
    own, far = lax.optimization_barrier((pack, far))
    mate = send(own, swap_core)
    forwarded = send(far, swap_core)

    places = jnp.asarray(position_tables())
    places = jnp.where(parity == 1, places[1], places[0])
    onehot = (places[:, None] == jnp.arange(256, dtype=jnp.int32)[None, :]).astype(BF)
    tick = call(tick_kernel, shape(8, 128), [ANY], flops=8 * 10**9, name="tick")(norm_b)

    def run_qkv(group, norms, parts):
        return call(
            functools.partial(qkv_kernel, group),
            [shape(2, 8, 80, 256)] * 3
            + [shape(D, 512), shape(256, D)]
            + [shape(2, 2, 288, 144, dtype=F32), shape(2, 2, 2, 160, 160, dtype=F32)],
            [VMEM] * 4 + [ANY] + [VMEM] * 2,
            [pltpu.VMEM((D, 256), BF)] + [pltpu.VMEM((128, 256), BF)] * 2,
            flops=2 * 10**9,
            name="qkv_" + str(group),
        )(*norms, onehot[:304], onehot[304:], tick, *parts)

    near = run_qkv(0, (norm_a, norm_b), (own, far))
    up, down = call(
        fetch_kernel, [shape(D, 2048), shape(2048, D)], [HBM] * 3,
        [pltpu.SemaphoreType.DMA((2,))], flops=10**9, name="fetch",
    )(up_weight, down_weight, near[3])
    rest = run_qkv(1, (norm_a, norm_b), (mate, forwarded))
    heads = near[:6] + rest[:6]

    def run_half(half, remote, resid):
        return call(
            functools.partial(half_kernel, half),
            [shape(4, 6, 24, D, dtype=F32), shape(2, 2, 80, 256), shape(2, 2, 80, 256)],
            [VMEM] * 17,
            [
                pltpu.VMEM((6, 144, 256), BF), pltpu.VMEM((6, 144, 256), BF),
                pltpu.VMEM((2, 432, 256), F32), pltpu.VMEM((432, 2048), BF),
                pltpu.VMEM((432, D), F32),
            ],
            flops=4 * 10**9,
            name="half_" + "ab"[half],
        )(remote, resid, gain_mlp, up, down, *heads)

    inner_b, key_b, value_b = run_half(1, remote_b, resid_b)
    def run_gather(blocks, after, name):
        first, second = call(
            functools.partial(gather_kernel, len(blocks)),
            [shape(80 * len(blocks), D)] * 2, [VMEM] * len(blocks) + [ANY], name=name,
        )(*blocks, after)
        return send(first, swap_core), send(second, swap_chip)

    first, second = run_gather((norm_b, remote_b, norm_a, remote_a), key_b, "gather")
    inner_a, key_a, value_a = run_half(0, remote_a, resid_a)

    remotes = (key_a, value_a, key_b, value_b)
    edge_heads = (*near[:5], near[6], *rest[:5], rest[6])
    before = call(
        first_edge_kernel,
        shape(2, 144, 256, dtype=F32),
        [VMEM] * 17,
        [pltpu.VMEM((320, 512), F32)],
        flops=10**9,
        name="edge_first",
    )(first, *remotes, *edge_heads)
    out = call(
        edge_kernel,
        shape(4, 2, 6, 24, D),
        [VMEM] * 25,
        [
            pltpu.VMEM((320, 512), F32), pltpu.VMEM((2, 288, 256), F32), pltpu.VMEM((288, D), F32),
            pltpu.VMEM((2, 144, D), F32), pltpu.VMEM((2, 4, 6, 24, D), BF), pltpu.VMEM((288, 2048), BF),
            pltpu.SemaphoreType.DMA((8,)),
        ],
        out_specs=ANY,
        flops=4 * 10**9,
        name="edge",
    )(second, *remotes, before, resid_a, resid_b, gain_mlp, inner_a, inner_b, up, down, *edge_heads)
    return out.reshape(4, 12, 24, D).transpose(0, 2, 1, 3)


def solution(mesh):
    in_specs = (
        P(None, "head", "tile", None),
        P("head", "tile"),
        P(),
        P(),
        P(None, None, "head"),
        P("head", None),
        P("head", None, None),
        P("head", None, None),
        P(),
        P(),
        P(),
    )
    out_specs = P(None, "head", "tile", None)
    return jax.shard_map(shards, mesh=mesh, in_specs=in_specs, out_specs=out_specs, check_vma=False)
```
